128 devices in a mesh: gx: 16 (over y, x_lo, core), gy: 8 (over x_hi, z).
Axes of the slice: x: 4 (x_hi: 2, x_lo: 2; x = x_hi * 2 + x_lo), y: 4, z: 4, core: 2. Of those that a mesh axis runs over, the one named last changes fastest.
Arguments:
- fields: float32 [4, 16, 512, 1024], P(None, None, 'gx', 'gy'), may hold values from -4 to 4
- solid_mask: int32 [16, 512, 1024], P(None, 'gx', 'gy'), may hold values 0 or 1
Outputs:
- advanced: float32 [4, 16, 512, 1024], P(None, None, 'gx', 'gy')
The draws below stay inside these ranges and needn't reach their ends.
Inputs may be any that keep to these rules, and one draw needn't show every extreme that they name: `solid_mask`: 1 marks a solid voxel, 0 a pore voxel.
All inputs are finite; a program needn't handle non-finite values. No bound on the sum of `solid_mask` on one device may be relied on, other than what follows from the above.
Results may differ from the reference program's by a relative error of at most 0.00002.
Values sent between devices are 32-bit elements; how exact they have to be, the bound alone decides.
No kernel may reach another device: no remote copies, remote signals or barrier semaphores. Data moves between devices by JAX's collectives and lax.ppermute only.
A program may use at most 192 MiB of HBM per device.

```python
import jax
import jax.numpy as jnp

NZ = 16
STEPS = 2
NX = 512
NY = 1024


def plant(values, key, low, high):
    index_at = [jax.random.randint(jax.random.fold_in(key, axis), (), 0, length) for axis, length in enumerate(values.shape)]
    longest = values.shape.index(max(values.shape))
    neighbour = index_at[:longest] + [(index_at[longest] + 1) % values.shape[longest]] + index_at[longest + 1:]
    return values.at[tuple(index_at)].set(low).at[tuple(neighbour)].set(high)


def level_of(stream_key, shape, pieces, low, largest):
    factor_of = 1.0
    for position, parts in pieces:
        draws = jax.random.uniform(jax.random.fold_in(jax.random.fold_in(stream_key, 6), position), (parts,), jnp.float32, low / len(pieces), largest / len(pieces))
        factor_of = factor_of * jnp.repeat(jnp.exp(draws), shape[position] // parts).reshape((-1,) + (1,) * (len(shape) - 1 - position))
    return factor_of


def noise(stream_key, shape, spread, reach, cuts=(), held_as=jnp.bfloat16):
    loudness = level_of(stream_key, shape, cuts, -0.22, 0.18) if cuts else 1.0
    values = jax.random.normal(stream_key, shape, jnp.float32) * spread * loudness
    return jnp.minimum(jnp.maximum(values, -reach), reach).astype(held_as)


def setup_inputs(seed: int = 0) -> dict:
    splits = jax.random.split(jax.random.key(seed), 3)
    return {
        "fields": noise(splits[0], (4, NZ, NX, NY), 0.5, 4.0, ((2, 16), (3, 8)), jnp.float32),
        "solid_mask": plant((jax.random.randint(splits[1], (NZ, NX, NY), 0, 5) < 3).astype(jnp.int32), jax.random.fold_in(splits[1], 1), 0, 1),
    }


viscosity = 0.05
penalty = 10.0
forcing = 0.5
sound_sq = 2.25
time_step = 0.2


def shifted(array, axis, offset):
    return jnp.roll(array, -offset, axis=axis)


def first_diff(array, axis):
    return (8.0 * (shifted(array, axis, 1) - shifted(array, axis, -1)) - (shifted(array, axis, 2) - shifted(array, axis, -2))) / 12.0


def second_diff(array, axis):
    return (16.0 * (shifted(array, axis, 1) + shifted(array, axis, -1)) - (shifted(array, axis, 2) + shifted(array, axis, -2)) - 30.0 * array) / 12.0


def combine(center, grad_z, grad_x, grad_y, laplace, solid):
    speed = center[0:3]
    advect = center[0] * grad_x[0:3] + center[1] * grad_y[0:3] + center[2] * grad_z[0:3]
    pressure_grad = jnp.stack([grad_x[3], grad_y[3], grad_z[3]])
    drive = jnp.array([forcing, 0.0, 0.0], jnp.float32)[:, None, None, None]
    momentum = -advect - pressure_grad + viscosity * laplace - penalty * solid * speed + drive
    pressure = -sound_sq * (grad_x[0] + grad_y[1] + grad_z[2])
    return jnp.concatenate([momentum, pressure[None]], axis=0)


def tendency(state, solid):
    grad_z = first_diff(state, 1)
    grad_x = first_diff(state, 2)
    grad_y = first_diff(state, 3)
    speed = state[0:3]
    laplace = second_diff(speed, 1) + second_diff(speed, 2) + second_diff(speed, 3)
    return combine(state, grad_z, grad_x, grad_y, laplace, solid)


def reference(fields, solid_mask):
    solid = solid_mask.astype(jnp.float32)
    state = fields
    for step in range(STEPS):
        section_one = state + time_step * tendency(state, solid)
        section_two = 0.75 * state + 0.25 * (section_one + time_step * tendency(section_one, solid))
        state = state / 3.0 + (2.0 / 3.0) * (section_two + time_step * tendency(section_two, solid))
    return state
```

```python
import jax
import jax.numpy as jnp
from jax import lax
from jax.sharding import PartitionSpec as P
from jax.experimental import pallas as pl
from jax.experimental.pallas import tpu as pltpu

STAGES = 6
DEPTH = 2 * STAGES
viscosity = 0.05
penalty = 10.0
forcing = 0.5
sound_sq = 2.25
time_step = 0.2

NF, NZ, NX, NY = 4, 16, 32, 128
ROWS = 64
OWN = 16
TOP = OWN - DEPTH
BOTTOM = OWN + NX
F32 = jnp.float32


def lanes(shape):
    return lax.broadcasted_iota(jnp.int32, shape, len(shape) - 1)


def pack_kernel(par_ref, q_ref, m_ref, xa_ref, xb_ref, ya_ref, yb_ref):
    px = par_ref[0]
    py = par_ref[1]

    def rows_to(dst, start):
        dst[0:NF] = q_ref[:, :, start:start + DEPTH, :]
        dst[NF] = m_ref[:, start:start + DEPTH, :].astype(F32)

    @pl.when(px == 0)
    def _():
        rows_to(xa_ref, NX - DEPTH)
        rows_to(xb_ref, 0)

    @pl.when(px == 1)
    def _():
        rows_to(xa_ref, 0)
        rows_to(xb_ref, NX - DEPTH)

    lane = lanes((NX, NY))
    group = lane // 32
    low = lane % 32 < 16
    even = py == 0

    def field(f, load):
        def packed(zi):
            out = pltpu.roll(load(zi), 16, 1)
            for zq in range(1, 4):
                out = jnp.where(group == zq, pltpu.roll(load(4 * zq + zi), (16 + 32 * zq) % NY, 1), out)
            return out
        for h in range(2):
            first, second = packed(h), packed(h + 2)
            right = jnp.where(low, first, pltpu.roll(second, 16, 1))
            left = jnp.where(low, pltpu.roll(second, NY - 16, 1), first)
            ya_ref[f, h] = jnp.where(even, right, left)
            yb_ref[f, h] = jnp.where(even, left, right)

    for f in range(NF):
        field(f, lambda z, f=f: q_ref[f, z])
    field(NF, lambda z: m_ref[z].astype(F32))


def strip_kernel(par_ref, ya_ref, yb_ref, t_ref, xa_ref, xb_ref):
    px = par_ref[0]
    even = par_ref[1] == 0
    low = lanes((NX, NY)) % 32 < 16
    for f in range(NF + 1):
        for h in range(2):
            a = ya_ref[f, h]
            b = yb_ref[f, h]
            left = jnp.where(even, b, a)
            right = jnp.where(even, a, b)
            t_ref[f, h] = jnp.where(low, left, right)
            t_ref[f, h + 2] = jnp.where(low, pltpu.roll(left, NY - 16, 1), pltpu.roll(right, 16, 1))

    @pl.when(px == 0)
    def _():
        xa_ref[...] = t_ref[:, :, NX - DEPTH:, :]
        xb_ref[...] = t_ref[:, :, :DEPTH, :]

    @pl.when(px == 1)
    def _():
        xa_ref[...] = t_ref[:, :, :DEPTH, :]
        xb_ref[...] = t_ref[:, :, NX - DEPTH:, :]


def update(alpha, beta, center, around, base, solid):
    scale = beta * time_step * 2.0 / 3.0
    nu = beta * viscosity * time_step / 12.0
    u, v, w, p = center
    speed = [-scale * u, -scale * v, -scale * w]
    keep = beta - 90.0 * nu - (beta * time_step * penalty) * solid
    out = []
    p_diff = []
    for plus, minus, plus2, minus2 in around(3):
        p_diff.append((plus - minus) - 0.125 * (plus2 - minus2))
    divergence = None
    for k in range(3):
        near = far = None
        total = center[k] * keep - scale * p_diff[k]
        for d, (plus, minus, plus2, minus2) in enumerate(around(k)):
            diff = (plus - minus) - 0.125 * (plus2 - minus2)
            total = total + speed[d] * diff
            s1, s2 = plus + minus, plus2 + minus2
            near = s1 if near is None else near + s1
            far = s2 if far is None else far + s2
            if d == k:
                divergence = diff if divergence is None else divergence + diff
        total = total + ((16.0 * nu) * near - nu * far)
        if k == 0:
            total = total + beta * time_step * forcing
        out.append(total)
    out.append(beta * p - (sound_sq * scale) * divergence)
    if alpha:
        out = [o + alpha * base(f) for f, o in enumerate(out)]
    return out


def main_kernel(par_ref, q_in, m_in, xa_ref, xb_ref, t_in, ca_ref, cb_ref, out_ref,
                q, s1, s2, solid, tq, t1, t2, tsolid):
    px = par_ref[0]
    lane8 = lanes((8, NY))
    piece = lane8 % 32
    group = lane8 // 32

    for f in range(NF):
        q[f, :, OWN:BOTTOM, :] = q_in[f]
        tq[f, 2:6, OWN:BOTTOM, :] = t_in[f]
    solid[:, OWN:BOTTOM, :] = m_in[...].astype(F32)
    tsolid[:, OWN:BOTTOM, :] = t_in[NF]

    def halos(top, bottom, ctop, cbottom):
        q[:, :, TOP:OWN, :] = top[0:NF]
        q[:, :, BOTTOM:BOTTOM + DEPTH, :] = bottom[0:NF]
        solid[:, TOP:OWN, :] = top[NF]
        solid[:, BOTTOM:BOTTOM + DEPTH, :] = bottom[NF]
        tq[:, 2:6, TOP:OWN, :] = ctop[0:NF]
        tq[:, 2:6, BOTTOM:BOTTOM + DEPTH, :] = cbottom[0:NF]
        tsolid[:, TOP:OWN, :] = ctop[NF]
        tsolid[:, BOTTOM:BOTTOM + DEPTH, :] = cbottom[NF]

    @pl.when(px == 0)
    def _():
        halos(xb_ref, xa_ref, cb_ref, ca_ref)

    @pl.when(px == 1)
    def _():
        halos(xa_ref, xb_ref, ca_ref, cb_ref)

    for f in range(NF):
        for r in range(0, ROWS, 8):
            rr = pl.ds(r, 8)
            for zi in range(4):
                tq[f, (zi + 6) % 8, rr, :] = pltpu.roll(tq[f, zi + 2, rr, :], 96 if zi < 2 else 32, 1)

    def stage(number, cur, tcur, base, tbase, out, tout, alpha, beta):
        start = TOP + 2 * number
        stop = BOTTOM + DEPTH - 2 * number
        tiles = list(range(start, stop, 8))
        last = number == STAGES

        def strips(zi, carry):
            for r in tiles:
                rr = pl.ds(r, 8)

                def around(f):
                    a = tcur[f, zi + 2, rr, :]
                    c = pltpu.roll(cur[f, zi, rr, :], 16, 1)
                    for zq in range(1, 4):
                        c = jnp.where(group == zq, pltpu.roll(cur[f, 4 * zq + zi, rr, :], (16 + 32 * zq) % NY, 1), c)
                    yp = pltpu.roll(jnp.where(piece == 16, c, a), NY - 1, 1)
                    ym = pltpu.roll(jnp.where(piece == 15, c, a), 1, 1)
                    yp2 = pltpu.roll(jnp.where((piece == 16) | (piece == 17), c, a), NY - 2, 1)
                    ym2 = pltpu.roll(jnp.where((piece == 14) | (piece == 15), c, a), 2, 1)
                    x = [tcur[f, zi + 2, pl.ds(r + o, 8), :] for o in (1, -1, 2, -2)]
                    z = [tcur[f, zi + 2 + o, rr, :] for o in (1, -1, 2, -2)]
                    return x, (yp, ym, yp2, ym2), z

                center = [tcur[f, zi + 2, rr, :] for f in range(NF)]
                new = update(alpha, beta, center, around,
                             lambda f: tbase[f, zi + 2, rr, :], tsolid[zi, rr, :])
                ghost = lax.rem(zi + 6, 8)
                turn = jnp.where(zi < 2, 96, 32)
                for f in range(NF):
                    tout[f, zi + 2, rr, :] = new[f]
                    tout[f, ghost, rr, :] = pltpu.roll(new[f], turn, 1)
            return carry

        def main(z, carry):
            zi = lax.rem(z, 4)
            turn = 112 - 32 * (z // 4)
            zs = [lax.rem(z + o, NZ) for o in (1, NZ - 1, 2, NZ - 2)]
            for r in tiles:
                rr = pl.ds(r, 8)

                def around(f):
                    a = cur[f, z, rr, :]
                    e = pltpu.roll(tcur[f, zi + 2, rr, :], turn, 1)
                    yp = pltpu.roll(jnp.where(lane8 == 0, e, a), NY - 1, 1)
                    ym = pltpu.roll(jnp.where(lane8 == NY - 1, e, a), 1, 1)
                    yp2 = pltpu.roll(jnp.where(lane8 < 2, e, a), NY - 2, 1)
                    ym2 = pltpu.roll(jnp.where(lane8 >= NY - 2, e, a), 2, 1)
                    x = [cur[f, z, pl.ds(r + o, 8), :] for o in (1, -1, 2, -2)]
                    zz = [cur[f, k, rr, :] for k in zs]
                    return x, (yp, ym, yp2, ym2), zz

                center = [cur[f, z, rr, :] for f in range(NF)]
                new = update(alpha, beta, center, around,
                             lambda f: base[f, z, rr, :], solid[z, rr, :])
                for f in range(NF):
                    if last:
                        out_ref[f, z, pl.ds(r - OWN, 8), :] = new[f]
                    else:
                        out[f, z, rr, :] = new[f]
            return carry

        if not last:
            lax.fori_loop(0, 4, strips, 0)
        lax.fori_loop(0, NZ, main, 0)

    for step in range(2):
        stage(3 * step + 1, q, tq, q, tq, s1, t1, 0.0, 1.0)
        stage(3 * step + 2, s1, t1, q, tq, s2, t2, 0.75, 0.25)
        stage(3 * step + 3, s2, t2, q, tq, q, tq, 1.0 / 3.0, 2.0 / 3.0)


def call(kernel, outs, scratch=(), scalars=1, inputs=0):
    vmem = pl.BlockSpec(memory_space=pltpu.VMEM)
    return pl.pallas_call(
        kernel,
        out_shape=[jax.ShapeDtypeStruct(s, F32) for s in outs],
        in_specs=[pl.BlockSpec(memory_space=pltpu.SMEM)] * scalars + [vmem] * inputs,
        out_specs=[vmem] * len(outs),
        scratch_shapes=[pltpu.VMEM(s, F32) for s in scratch],
        compiler_params=pltpu.CompilerParams(vmem_limit_bytes=48 * 2 ** 20),
    )


def solution(mesh):
    nx, ny = mesh.shape["gx"], mesh.shape["gy"]

    def pairs(count, parity):
        return [(i, (i + 1) % count if i % 2 == parity else (i - 1) % count) for i in range(count)]

    def body(fields, solid_mask):
        parity = jnp.stack([lax.axis_index("gx") % 2, lax.axis_index("gy") % 2]).astype(jnp.int32)
        xmsg = (NF + 1, NZ, DEPTH, NY)
        ymsg = (NF + 1, 2, NX, NY)
        strip = (NF + 1, 4, NX, NY)
        cmsg = (NF + 1, 4, DEPTH, NY)
        xa, xb, ya, yb = call(pack_kernel, [xmsg, xmsg, ymsg, ymsg], inputs=2)(parity, fields, solid_mask)
        xb = lax.ppermute(xb, "gx", pairs(nx, 1))
        yb = lax.ppermute(yb, "gy", pairs(ny, 1))
        ya = lax.ppermute(ya, "gy", pairs(ny, 0))
        xa = lax.ppermute(xa, "gx", pairs(nx, 0))
        t, ca, cb = call(strip_kernel, [strip, cmsg, cmsg], inputs=2)(parity, ya, yb)
        cb = lax.ppermute(cb, "gx", pairs(nx, 1))
        ca = lax.ppermute(ca, "gx", pairs(nx, 0))
        wide = (NF, NZ, ROWS, NY)
        narrow = (NF, 8, ROWS, NY)
        scratch = [wide] * 3 + [(NZ, ROWS, NY)] + [narrow] * 3 + [(4, ROWS, NY)]
        out, = call(main_kernel, [(NF, NZ, NX, NY)], scratch, inputs=7)(
            parity, fields, solid_mask, xa, xb, t, ca, cb)
        return out

    return jax.shard_map(
        body,
        mesh=mesh,
        in_specs=(P(None, None, "gx", "gy"), P(None, "gx", "gy")),
        out_specs=P(None, None, "gx", "gy"),
        check_vma=False,
    )
```

```python
import functools

import jax
import jax.numpy as jnp
import numpy as np
from jax import lax
from jax.sharding import PartitionSpec as P
from jax.experimental import pallas as pl
from jax.experimental.pallas import tpu as pltpu

STAGES = 6
DEPTH = 2 * STAGES
viscosity = 0.05
penalty = 10.0
forcing = 0.5
sound_sq = 2.25
time_step = 0.2

NF, NZ, NX, NY = 4, 16, 32, 128
ROWS = 64
OWN = 16
TOP = OWN - DEPTH
BOTTOM = OWN + NX
F32 = jnp.float32


def lanes(shape):
    return lax.broadcasted_iota(jnp.int32, shape, len(shape) - 1)


def pack_kernel(par_ref, q_ref, m_ref, xa_ref, xb_ref, ya_ref, yb_ref):
    px = par_ref[0]
    py = par_ref[1]

    def rows_to(dst, start):
        dst[0:NF] = q_ref[:, :, start:start + DEPTH, :]
        dst[NF] = m_ref[:, start:start + DEPTH, :].astype(F32)

    @pl.when(px == 0)
    def _():
        rows_to(xa_ref, NX - DEPTH)
        rows_to(xb_ref, 0)

    @pl.when(px == 1)
    def _():
        rows_to(xa_ref, 0)
        rows_to(xb_ref, NX - DEPTH)

    lane = lanes((NX, NY))
    group = lane // 32
    low = lane % 32 < 16
    even = py == 0

    def field(f, load):
        def packed(zi):
            out = pltpu.roll(load(zi), 16, 1)
            for zq in range(1, 4):
                out = jnp.where(group == zq, pltpu.roll(load(4 * zq + zi), (16 + 32 * zq) % NY, 1), out)
            return out
        for h in range(2):
            first, second = packed(h), packed(h + 2)
            right = jnp.where(low, first, pltpu.roll(second, 16, 1))
            left = jnp.where(low, pltpu.roll(second, NY - 16, 1), first)
            ya_ref[f, h] = jnp.where(even, right, left)
            yb_ref[f, h] = jnp.where(even, left, right)

    for f in range(NF):
        field(f, lambda z, f=f: q_ref[f, z])
    field(NF, lambda z: m_ref[z].astype(F32))


def strip_kernel(par_ref, ya_ref, yb_ref, t_ref, xa_ref, xb_ref):
    px = par_ref[0]
    even = par_ref[1] == 0
    low = lanes((NX, NY)) % 32 < 16
    for f in range(NF + 1):
        for h in range(2):
            a = ya_ref[f, h]
            b = yb_ref[f, h]
            left = jnp.where(even, b, a)
            right = jnp.where(even, a, b)
            t_ref[f, h] = jnp.where(low, left, right)
            t_ref[f, h + 2] = jnp.where(low, pltpu.roll(left, NY - 16, 1), pltpu.roll(right, 16, 1))

    @pl.when(px == 0)
    def _():
        xa_ref[...] = t_ref[:, :, NX - DEPTH:, :]
        xb_ref[...] = t_ref[:, :, :DEPTH, :]

    @pl.when(px == 1)
    def _():
        xa_ref[...] = t_ref[:, :, :DEPTH, :]
        xb_ref[...] = t_ref[:, :, NX - DEPTH:, :]


def update(alpha, beta, center, around, base, solid):
    scale = beta * time_step * 2.0 / 3.0
    nu = beta * viscosity * time_step / 12.0
    u, v, w, p = center
    speed = [-scale * u, -scale * v, -scale * w]
    keep = beta - 90.0 * nu - (beta * time_step * penalty) * solid

    def first(plus, minus, plus2, minus2):
        return (plus - minus) - 0.125 * (plus2 - minus2)

    out = []
    x, z, dy, _ = around(3)
    p_diff = [first(*x), dy, first(*z)]
    divergence = None
    for k in range(3):
        x, z, dy, sy = around(k)
        diffs = [first(*x), dy, first(*z)]
        near = (x[0] + x[1]) + (z[0] + z[1])
        far = (x[2] + x[3]) + (z[2] + z[3])
        total = center[k] * keep - scale * p_diff[k]
        for d in range(3):
            total = total + speed[d] * diffs[d]
        divergence = diffs[k] if divergence is None else divergence + diffs[k]
        total = total + nu * ((16.0 * near - far) + sy)
        if k == 0:
            total = total + beta * time_step * forcing
        out.append(total)
    out.append(beta * p - (sound_sq * scale) * divergence)
    if alpha:
        out = [o + alpha * base(f) for f, o in enumerate(out)]
    return out


def y_weights():
    taps = [(1, 1.0, 16.0), (-1, -1.0, 16.0), (2, -0.125, -1.0), (-2, 0.125, -1.0)]
    wide = np.zeros((4, 512, 256), np.float32)
    strip = np.zeros((1280, 256), np.float32)
    for o, first, second in taps:
        for j in range(NY):
            for zq in range(4):
                c = j + o
                if 0 <= c < NY:
                    rows = (c, c + 128)
                else:
                    lane = 32 * zq + 16 + (c if c < 0 else c - NY)
                    rows = (256 + lane, 384 + lane)
                for r in rows:
                    wide[zq, r, j] = first
                    wide[zq, r, j + NY] = second
            g, place = j // 32, j % 32
            c = place - 16 if place < 16 else NY + place - 16
            left = place < 16
            c += o
            if c < -16 or c >= NY + 16:
                continue
            if (left and c < 0) or (not left and c >= NY):
                lane = 32 * g + 16 + (c if c < 0 else c - NY)
                rows = (lane, lane + 128)
            else:
                rows = (256 + 256 * g + c, 384 + 256 * g + c)
            for r in rows:
                strip[r, j] = first
                strip[r, j + NY] = second
    return jnp.asarray(wide, jnp.bfloat16), jnp.asarray(strip, jnp.bfloat16)


def split(a):
    high = a.astype(jnp.bfloat16)
    return high, (a - high.astype(F32)).astype(jnp.bfloat16)


def main_kernel(par_ref, q_in, m_in, xa_ref, xb_ref, t_in, ca_ref, cb_ref, w_ref, ws_ref, out_ref,
                q, s1, s2, solid, tq, t1, t2, tsolid, yd, ytd):
    px = par_ref[0]

    for f in range(NF):
        q[f, :, OWN:BOTTOM, :] = q_in[f]
        tq[f, 2:6, OWN:BOTTOM, :] = t_in[f]
    solid[:, OWN:BOTTOM, :] = m_in[...].astype(F32)
    tsolid[:, OWN:BOTTOM, :] = t_in[NF]

    def halos(top, bottom, ctop, cbottom):
        q[:, :, TOP:OWN, :] = top[0:NF]
        q[:, :, BOTTOM:BOTTOM + DEPTH, :] = bottom[0:NF]
        solid[:, TOP:OWN, :] = top[NF]
        solid[:, BOTTOM:BOTTOM + DEPTH, :] = bottom[NF]
        tq[:, 2:6, TOP:OWN, :] = ctop[0:NF]
        tq[:, 2:6, BOTTOM:BOTTOM + DEPTH, :] = cbottom[0:NF]
        tsolid[:, TOP:OWN, :] = ctop[NF]
        tsolid[:, BOTTOM:BOTTOM + DEPTH, :] = cbottom[NF]

    @pl.when(px == 0)
    def _():
        halos(xb_ref, xa_ref, cb_ref, ca_ref)

    @pl.when(px == 1)
    def _():
        halos(xa_ref, xb_ref, ca_ref, cb_ref)

    for f in range(NF):
        for r in range(0, ROWS, 8):
            rr = pl.ds(r, 8)
            for zi in range(4):
                tq[f, (zi + 6) % 8, rr, :] = pltpu.roll(tq[f, zi + 2, rr, :], 96 if zi < 2 else 32, 1)

    def stage(number, cur, tcur, base, tbase, out, tout, alpha, beta):
        start = TOP + 2 * number
        stop = BOTTOM + DEPTH - 2 * number
        tiles = list(range(start, stop, 8))
        count = 8 * len(tiles)
        last = number == STAGES

        def along_y(f, carry):
            rr = pl.ds(start, count)

            def flat(ref, z):
                return split(ref[f, z:z + 4, rr, :].reshape(4 * count, NY))

            t = flat(tcur, 2)
            every = list(t)
            for zq in range(4):
                a = flat(cur, 4 * zq)
                every += a
                y = jnp.dot(jnp.concatenate(a + t, axis=1), w_ref[zq], preferred_element_type=F32)
                yd[f, 4 * zq:4 * zq + 4, 0:count, :] = y.reshape(4, count, 2 * NY)
            if not last:
                y = jnp.dot(jnp.concatenate(every, axis=1), ws_ref[...], preferred_element_type=F32)
                ytd[f, :, 0:count, :] = y.reshape(4, count, 2 * NY)
            return carry

        lax.fori_loop(0, NF, along_y, 0)

        def strips(half, zi, carry):
            for r in tiles:
                rr = pl.ds(r, 8)
                yr = pl.ds(r - start, 8)

                def around(f):
                    x = [tcur[f, zi + 2, pl.ds(r + o, 8), :] for o in (1, -1, 2, -2)]
                    z = [tcur[f, zi + 2 + o, rr, :] for o in (1, -1, 2, -2)]
                    return x, z, ytd[f, zi, yr, 0:NY], ytd[f, zi, yr, NY:]

                center = [tcur[f, zi + 2, rr, :] for f in range(NF)]
                new = update(alpha, beta, center, around,
                             lambda f: tbase[f, zi + 2, rr, :], tsolid[zi, rr, :])
                for f in range(NF):
                    tout[f, zi + 2, rr, :] = new[f]
                    tout[f, zi + (6 if half == 0 else -2), rr, :] = pltpu.roll(new[f], 32 if half else 96, 1)
            return carry

        def main(z, carry):
            zs = [lax.rem(z + o, NZ) for o in (1, NZ - 1, 2, NZ - 2)]
            for r in tiles:
                rr = pl.ds(r, 8)
                yr = pl.ds(r - start, 8)

                def around(f):
                    x = [cur[f, z, pl.ds(r + o, 8), :] for o in (1, -1, 2, -2)]
                    zz = [cur[f, k, rr, :] for k in zs]
                    return x, zz, yd[f, z, yr, 0:NY], yd[f, z, yr, NY:]

                center = [cur[f, z, rr, :] for f in range(NF)]
                new = update(alpha, beta, center, around,
                             lambda f: base[f, z, rr, :], solid[z, rr, :])
                for f in range(NF):
                    if last:
                        out_ref[f, z, pl.ds(r - OWN, 8), :] = new[f]
                    else:
                        out[f, z, rr, :] = new[f]
            return carry

        if not last:
            for half in range(2):
                lax.fori_loop(2 * half, 2 * half + 2, functools.partial(strips, half), 0)
        lax.fori_loop(0, NZ, main, 0)

    for step in range(2):
        stage(3 * step + 1, q, tq, q, tq, s1, t1, 0.0, 1.0)
        stage(3 * step + 2, s1, t1, q, tq, s2, t2, 0.75, 0.25)
        stage(3 * step + 3, s2, t2, q, tq, q, tq, 1.0 / 3.0, 2.0 / 3.0)


def call(kernel, outs, scratch=(), scalars=1, inputs=0):
    vmem = pl.BlockSpec(memory_space=pltpu.VMEM)
    return pl.pallas_call(
        kernel,
        out_shape=[jax.ShapeDtypeStruct(s, F32) for s in outs],
        in_specs=[pl.BlockSpec(memory_space=pltpu.SMEM)] * scalars + [vmem] * inputs,
        out_specs=[vmem] * len(outs),
        scratch_shapes=[pltpu.VMEM(s, F32) for s in scratch],
        compiler_params=pltpu.CompilerParams(vmem_limit_bytes=48 * 2 ** 20),
    )


def solution(mesh):
    nx, ny = mesh.shape["gx"], mesh.shape["gy"]

    def pairs(count, parity):
        return [(i, (i + 1) % count if i % 2 == parity else (i - 1) % count) for i in range(count)]

    def body(fields, solid_mask):
        parity = jnp.stack([lax.axis_index("gx") % 2, lax.axis_index("gy") % 2]).astype(jnp.int32)
        xmsg = (NF + 1, NZ, DEPTH, NY)
        ymsg = (NF + 1, 2, NX, NY)
        strip = (NF + 1, 4, NX, NY)
        cmsg = (NF + 1, 4, DEPTH, NY)
        xa, xb, ya, yb = call(pack_kernel, [xmsg, xmsg, ymsg, ymsg], inputs=2)(parity, fields, solid_mask)
        xb = lax.ppermute(xb, "gx", pairs(nx, 1))
        yb = lax.ppermute(yb, "gy", pairs(ny, 1))
        ya = lax.ppermute(ya, "gy", pairs(ny, 0))
        xa = lax.ppermute(xa, "gx", pairs(nx, 0))
        t, ca, cb = call(strip_kernel, [strip, cmsg, cmsg], inputs=2)(parity, ya, yb)
        cb = lax.ppermute(cb, "gx", pairs(nx, 1))
        ca = lax.ppermute(ca, "gx", pairs(nx, 0))
        wide = (NF, NZ, ROWS, NY)
        narrow = (NF, 8, ROWS, NY)
        scratch = [wide] * 3 + [(NZ, ROWS, NY)] + [narrow] * 3 + [(4, ROWS, NY)]
        scratch += [(NF, NZ, 56, 2 * NY), (NF, 4, 56, 2 * NY)]
        out, = call(main_kernel, [(NF, NZ, NX, NY)], scratch, inputs=9)(
            parity, fields, solid_mask, xa, xb, t, ca, cb, *y_weights())
        return out

    return jax.shard_map(
        body,
        mesh=mesh,
        in_specs=(P(None, None, "gx", "gy"), P(None, "gx", "gy")),
        out_specs=P(None, None, "gx", "gy"),
        check_vma=False,
    )
```

```python
import functools

import jax
import jax.numpy as jnp
import numpy as np
from jax import lax
from jax.sharding import PartitionSpec as P
from jax.experimental import pallas as pl
from jax.experimental.pallas import tpu as pltpu

STAGES = 6
DEPTH = 2 * STAGES
viscosity = 0.05
penalty = 10.0
forcing = 0.5
sound_sq = 2.25
time_step = 0.2

NF, NZ, NX, NY = 4, 16, 32, 128
ROWS = 64
OWN = 16
TOP = OWN - DEPTH
BOTTOM = OWN + NX
MSG = (NF + 1) * DEPTH - 2
F32 = jnp.float32


def lanes(shape):
    return lax.broadcasted_iota(jnp.int32, shape, len(shape) - 1)


def pack_y_kernel(par_ref, q_hbm, m_hbm, ya_ref, yb_ref, q_ref, m_ref, sems):
    copies = [pltpu.make_async_copy(m_hbm, m_ref, sems.at[NF])]
    copies += [pltpu.make_async_copy(q_hbm.at[f], q_ref.at[f], sems.at[f]) for f in range(NF)]
    for copy in copies:
        copy.start()
    lane = lanes((NX, NY))
    group = lane // 32
    low = lane % 32 < 16
    even = par_ref[1] == 0

    def packed(load, zi):
        out = pltpu.roll(load(zi), 16, 1)
        for zq in range(1, 4):
            out = jnp.where(group == zq, pltpu.roll(load(4 * zq + zi), (16 + 32 * zq) % NY, 1), out)
        return out

    def both(load, h):
        first, second = packed(load, h), packed(load, h + 2)
        return (jnp.where(low, first, pltpu.roll(second, 16, 1)),
                jnp.where(low, pltpu.roll(second, NY - 16, 1), first))

    copies[0].wait()
    mask = [both(lambda z: m_ref[z].astype(F32), h) for h in range(2)]
    for f in range(NF):
        copies[1 + f].wait()
        for h in range(2):
            right, left = both(lambda z: q_ref[f, z], h)
            if f < 3:
                right = jnp.where(lane % 16 < 4, pltpu.roll(mask[h][0], NY - 4 - 4 * f, 1), right)
                left = jnp.where(lane % 16 >= 12, pltpu.roll(mask[h][1], 12 - 4 * f, 1), left)
            ya_ref[f, h] = jnp.where(even, right, left)
            yb_ref[f, h] = jnp.where(even, left, right)


def send_rows(px, layers, q_ref, m_ref, a_ref, b_refs):
    def put(dst, bottom, first, count):
        start = NX - DEPTH if bottom else 0
        mstart = NX - DEPTH + 2 if bottom else 0
        for z in range(count):
            for f in range(NF):
                dst[z * MSG + f * DEPTH:z * MSG + (f + 1) * DEPTH] = q_ref[f, first + z, start:start + DEPTH, :]
            dst[z * MSG + NF * DEPTH:(z + 1) * MSG] = m_ref[first + z, mstart:mstart + DEPTH - 2, :].astype(F32)

    def send(a_bottom):
        put(a_ref, a_bottom, 0, layers)
        part = layers // len(b_refs)
        for i, b_ref in enumerate(b_refs):
            put(b_ref, not a_bottom, i * part, part)

    pl.when(px == 0)(lambda: send(True))
    pl.when(px == 1)(lambda: send(False))


def pack_x_kernel(par_ref, q_ref, m_ref, xa_ref, xb_ref, xb2_ref):
    send_rows(par_ref[0], NZ, q_ref, m_ref, xa_ref, (xb_ref, xb2_ref))


def strip_kernel(par_ref, ya_ref, yb_ref, t_ref, ts_ref, xa_ref, xb_ref):
    even = par_ref[1] == 0
    lane = lanes((NX, NY))
    low = lane % 32 < 16
    place = lane % 16

    def put(h, left, right):
        yield h, jnp.where(low, left, right)
        yield h + 2, jnp.where(low, pltpu.roll(left, NY - 16, 1), pltpu.roll(right, 16, 1))

    for h in range(2):
        mleft = mright = jnp.zeros((NX, NY), F32)
        for f in range(NF):
            a = ya_ref[f, h]
            b = yb_ref[f, h]
            left = jnp.where(even, b, a)
            right = jnp.where(even, a, b)
            if f < 3:
                mleft = jnp.where(place // 4 == f + 1, pltpu.roll(left, 4 + 4 * f, 1), mleft)
                mright = jnp.where(place // 4 == f, pltpu.roll(right, NY - 12 + 4 * f, 1), mright)
            for zi, value in put(h, left, right):
                t_ref[f, zi] = value
        for zi, value in put(h, mleft, mright):
            ts_ref[zi] = value
    send_rows(par_ref[0], 4, t_ref, ts_ref, xa_ref, (xb_ref,))


def update(alpha, beta, center, around, base, solid):
    scale = beta * time_step * 2.0 / 3.0
    nu = beta * viscosity * time_step / 12.0
    u, v, w, p = center
    speed = [-scale * u, -scale * v, -scale * w]
    keep = beta - 90.0 * nu - (beta * time_step * penalty) * solid

    def first(plus, minus, plus2, minus2):
        return (plus - minus) - 0.125 * (plus2 - minus2)

    out = []
    x, z, dy, _ = around(3)
    p_diff = [first(*x), dy, first(*z)]
    divergence = None
    for k in range(3):
        x, z, dy, sy = around(k)
        diffs = [first(*x), dy, first(*z)]
        near = (x[0] + x[1]) + (z[0] + z[1])
        far = (x[2] + x[3]) + (z[2] + z[3])
        total = center[k] * keep - scale * p_diff[k]
        for d in range(3):
            total = total + speed[d] * diffs[d]
        divergence = diffs[k] if divergence is None else divergence + diffs[k]
        total = total + nu * ((16.0 * near - far) + sy)
        if k == 0:
            total = total + beta * time_step * forcing
        out.append(total)
    out.append(beta * p - (sound_sq * scale) * divergence)
    if alpha:
        out = [o + alpha * base(f) for f, o in enumerate(out)]
    return out


def y_weights():
    taps = [(1, 1.0, 16.0), (-1, -1.0, 16.0), (2, -0.125, -1.0), (-2, 0.125, -1.0)]
    wide = np.zeros((4, 512, 256), np.float32)
    strip = np.zeros((1280, 256), np.float32)
    for o, first, second in taps:
        for j in range(NY):
            for zq in range(4):
                c = j + o
                if 0 <= c < NY:
                    rows = (c, c + 128)
                else:
                    lane = 32 * zq + 16 + (c if c < 0 else c - NY)
                    rows = (256 + lane, 384 + lane)
                for r in rows:
                    wide[zq, r, j] = first
                    wide[zq, r, j + NY] = second
            g, place = j // 32, j % 32
            c = place - 16 if place < 16 else NY + place - 16
            left = place < 16
            c += o
            if c < -16 or c >= NY + 16:
                continue
            if (left and c < 0) or (not left and c >= NY):
                lane = 32 * g + 16 + (c if c < 0 else c - NY)
                rows = (lane, lane + 128)
            else:
                rows = (256 + 256 * g + c, 384 + 256 * g + c)
            for r in rows:
                strip[r, j] = first
                strip[r, j + NY] = second
    return jnp.asarray(wide, jnp.bfloat16), jnp.asarray(strip, jnp.bfloat16)


def split(a):
    high = a.astype(jnp.bfloat16)
    return high, (a - high.astype(F32)).astype(jnp.bfloat16)


def main_kernel(par_ref, q_in, m_in, xa_ref, xb_ref, xb2_ref, t_in, ts_in, ca_ref, cb_ref, w_ref, ws_ref, out_ref,
                q, s1, s2, solid, tq, t1, t2, tsolid, yd, ytd):
    px = par_ref[0]

    for f in range(NF):
        q[f, :, OWN:BOTTOM, :] = q_in[f]
        tq[f, 2:6, OWN:BOTTOM, :] = t_in[f]
    solid[:, OWN:BOTTOM, :] = m_in[...].astype(F32)
    tsolid[:, OWN:BOTTOM, :] = ts_in[...]

    def halo(msgs, layers, shift, fields, mask, top):
        row = TOP if top else BOTTOM
        mrow = TOP + 2 if top else BOTTOM
        part = layers // len(msgs)
        for z in range(layers):
            msg, at = msgs[z // part], z % part * MSG
            for f in range(NF):
                fields[f, z + shift, row:row + DEPTH, :] = msg[at + f * DEPTH:at + (f + 1) * DEPTH]
            mask[z, mrow:mrow + DEPTH - 2, :] = msg[at + NF * DEPTH:at + MSG]

    def halos(a_bottom):
        halo((xa_ref,), NZ, 0, q, solid, not a_bottom)
        halo((xb_ref, xb2_ref), NZ, 0, q, solid, a_bottom)
        halo((ca_ref,), 4, 2, tq, tsolid, not a_bottom)
        halo((cb_ref,), 4, 2, tq, tsolid, a_bottom)

    pl.when(px == 0)(lambda: halos(True))
    pl.when(px == 1)(lambda: halos(False))

    for f in range(NF):
        for r in range(0, ROWS, 8):
            rr = pl.ds(r, 8)
            for zi in range(4):
                tq[f, (zi + 6) % 8, rr, :] = pltpu.roll(tq[f, zi + 2, rr, :], 96 if zi < 2 else 32, 1)

    def stage(number, cur, tcur, base, tbase, out, tout, alpha, beta):
        start = TOP + 2 * number
        stop = BOTTOM + DEPTH - 2 * number
        tiles = list(range(start, stop, 8))
        count = 8 * len(tiles)
        last = number == STAGES

        def along_y(f, carry):
            rr = pl.ds(start, count)

            def flat(ref, z):
                return split(ref[f, z:z + 4, rr, :].reshape(4 * count, NY))

            t = flat(tcur, 2)
            every = list(t)
            for zq in range(4):
                a = flat(cur, 4 * zq)
                every += a
                y = jnp.dot(jnp.concatenate(a + t, axis=1), w_ref[zq], preferred_element_type=F32)
                yd[f, 4 * zq:4 * zq + 4, 0:count, :] = y.reshape(4, count, 2 * NY)
            if not last:
                y = jnp.dot(jnp.concatenate(every, axis=1), ws_ref[...], preferred_element_type=F32)
                ytd[f, :, 0:count, :] = y.reshape(4, count, 2 * NY)
            return carry

        lax.fori_loop(0, NF, along_y, 0)

        def strips(half, zi, carry):
            for r in tiles:
                rr = pl.ds(r, 8)
                yr = pl.ds(r - start, 8)

                def around(f):
                    x = [tcur[f, zi + 2, pl.ds(r + o, 8), :] for o in (1, -1, 2, -2)]
                    z = [tcur[f, zi + 2 + o, rr, :] for o in (1, -1, 2, -2)]
                    return x, z, ytd[f, zi, yr, 0:NY], ytd[f, zi, yr, NY:]

                center = [tcur[f, zi + 2, rr, :] for f in range(NF)]
                new = update(alpha, beta, center, around,
                             lambda f: tbase[f, zi + 2, rr, :], tsolid[zi, rr, :])
                for f in range(NF):
                    tout[f, zi + 2, rr, :] = new[f]
                    tout[f, zi + (6 if half == 0 else -2), rr, :] = pltpu.roll(new[f], 32 if half else 96, 1)
            return carry

        def main(z, carry):
            zs = [lax.rem(z + o, NZ) for o in (1, NZ - 1, 2, NZ - 2)]
            for r in tiles:
                rr = pl.ds(r, 8)
                yr = pl.ds(r - start, 8)

                def around(f):
                    x = [cur[f, z, pl.ds(r + o, 8), :] for o in (1, -1, 2, -2)]
                    zz = [cur[f, k, rr, :] for k in zs]
                    return x, zz, yd[f, z, yr, 0:NY], yd[f, z, yr, NY:]

                center = [cur[f, z, rr, :] for f in range(NF)]
                new = update(alpha, beta, center, around,
                             lambda f: base[f, z, rr, :], solid[z, rr, :])
                for f in range(NF):
                    if last:
                        out_ref[f, z, pl.ds(r - OWN, 8), :] = new[f]
                    else:
                        out[f, z, rr, :] = new[f]
            return carry

        if not last:
            for half in range(2):
                lax.fori_loop(2 * half, 2 * half + 2, functools.partial(strips, half), 0)
        lax.fori_loop(0, NZ, main, 0)

    for step in range(2):
        stage(3 * step + 1, q, tq, q, tq, s1, t1, 0.0, 1.0)
        stage(3 * step + 2, s1, t1, q, tq, s2, t2, 0.75, 0.25)
        stage(3 * step + 3, s2, t2, q, tq, q, tq, 1.0 / 3.0, 2.0 / 3.0)


def call(kernel, outs, scratch=(), inputs=0, hbm=0, where=pltpu.HBM):
    vmem = pl.BlockSpec(memory_space=pltpu.VMEM)
    specs = [pl.BlockSpec(memory_space=pltpu.SMEM)] + [pl.BlockSpec(memory_space=where)] * hbm + [vmem] * inputs
    return pl.pallas_call(
        kernel,
        out_shape=[jax.ShapeDtypeStruct(s, F32) for s in outs],
        in_specs=specs,
        out_specs=[vmem] * len(outs),
        scratch_shapes=list(scratch),
        compiler_params=pltpu.CompilerParams(vmem_limit_bytes=44 * 2 ** 20),
    )


def solution(mesh):
    nx, ny = mesh.shape["gx"], mesh.shape["gy"]

    def pairs(count, parity):
        return [(i, (i + 1) % count if i % 2 == parity else (i - 1) % count) for i in range(count)]

    def body(fields, solid_mask):
        parity = jnp.stack([lax.axis_index("gx") % 2, lax.axis_index("gy") % 2]).astype(jnp.int32)
        ymsg = (NF, 2, NX, NY)
        own = [pltpu.VMEM((NF, NZ, NX, NY), F32), pltpu.VMEM((NZ, NX, NY), jnp.int32),
               pltpu.SemaphoreType.DMA((NF + 1,))]
        ya, yb = call(pack_y_kernel, [ymsg, ymsg], own, hbm=2)(parity, fields, solid_mask)
        yb = lax.ppermute(yb, "gy", pairs(ny, 1))
        ya = lax.ppermute(ya, "gy", pairs(ny, 0))
        half = (NZ // 2 * MSG, NY)
        xa, xb, xb2 = call(pack_x_kernel, [(NZ * MSG, NY), half, half], inputs=2)(parity, fields, solid_mask)
        xb = lax.ppermute(xb, "gx", pairs(nx, 1))
        xb2 = lax.ppermute(xb2, "gx", pairs(nx, 1))
        xa = lax.ppermute(xa, "gx", pairs(nx, 0))
        t, ts, ca, cb = call(strip_kernel, [(NF, 4, NX, NY), (4, NX, NY), (4 * MSG, NY), (4 * MSG, NY)],
                             inputs=2)(parity, ya, yb)
        cb = lax.ppermute(cb, "gx", pairs(nx, 1))
        ca = lax.ppermute(ca, "gx", pairs(nx, 0))
        wide = (NF, NZ, ROWS, NY)
        narrow = (NF, 8, ROWS, NY)
        scratch = [wide] * 3 + [(NZ, ROWS, NY)] + [narrow] * 3 + [(4, ROWS, NY)]
        scratch += [(NF, NZ, 56, 2 * NY), (NF, 4, 56, 2 * NY)]
        out, = call(main_kernel, [(NF, NZ, NX, NY)], [pltpu.VMEM(s, F32) for s in scratch], inputs=11)(
            parity, fields, solid_mask, xa, xb, xb2, t, ts, ca, cb, *y_weights())
        return out

    return jax.shard_map(
        body,
        mesh=mesh,
        in_specs=(P(None, None, "gx", "gy"), P(None, "gx", "gy")),
        out_specs=P(None, None, "gx", "gy"),
        check_vma=False,
    )
```

```python
import functools

import jax
import jax.numpy as jnp
import numpy as np
from jax import lax
from jax.sharding import PartitionSpec as P
from jax.experimental import pallas as pl
from jax.experimental.pallas import tpu as pltpu

STAGES = 6
DEPTH = 2 * STAGES
viscosity = 0.05
penalty = 10.0
forcing = 0.5
sound_sq = 2.25
time_step = 0.2

NF, NZ, NX, NY = 4, 16, 32, 128
ROWS = 64
OWN = 16
TOP = OWN - DEPTH
BOTTOM = OWN + NX
MSG = (NF + 1) * DEPTH - 2
F32 = jnp.float32
FIRST = 8


def lanes(shape):
    return lax.broadcasted_iota(jnp.int32, shape, len(shape) - 1)


def send_rows(px, layers, q_ref, m_ref, a_ref, b_refs):
    def put(dst, bottom, first, count):
        start = NX - DEPTH if bottom else 0
        mstart = NX - DEPTH + 2 if bottom else 0
        for z in range(count):
            for f in range(NF):
                dst[z * MSG + f * DEPTH:z * MSG + (f + 1) * DEPTH] = q_ref[f, first + z, start:start + DEPTH, :]
            dst[z * MSG + NF * DEPTH:(z + 1) * MSG] = m_ref[first + z, mstart:mstart + DEPTH - 2, :].astype(F32)

    def send(a_bottom):
        put(a_ref, a_bottom, 0, layers)
        first = 0
        for b_ref in b_refs:
            count = b_ref.shape[0] // MSG
            put(b_ref, not a_bottom, first, count)
            first += count

    pl.when(px == 0)(lambda: send(True))
    pl.when(px == 1)(lambda: send(False))


def pack_kernel(par_ref, q_hbm, m_hbm, yb_ref, ya_ref, xa_ref, xb_ref, xb2_ref, q_ref, m_ref, sems):
    copies = [pltpu.make_async_copy(m_hbm, m_ref, sems.at[NF])]
    copies += [pltpu.make_async_copy(q_hbm.at[f], q_ref.at[f], sems.at[f]) for f in range(NF)]
    for copy in copies:
        copy.start()
    lane = lanes((NX, NY))
    group = lane // 32
    low = lane % 32 < 16
    even = par_ref[1] == 0

    def packed(load, zi):
        out = pltpu.roll(load(zi), 16, 1)
        for zq in range(1, 4):
            out = jnp.where(group == zq, pltpu.roll(load(4 * zq + zi), (16 + 32 * zq) % NY, 1), out)
        return out

    def both(load, h):
        first, second = packed(load, h), packed(load, h + 2)
        return (jnp.where(low, first, pltpu.roll(second, 16, 1)),
                jnp.where(low, pltpu.roll(second, NY - 16, 1), first))

    copies[0].wait()
    mask = [both(lambda z: m_ref[z].astype(F32), h) for h in range(2)]
    for f in range(NF):
        copies[1 + f].wait()
        for h in range(2):
            right, left = both(lambda z: q_ref[f, z], h)
            if f < 3:
                right = jnp.where(lane % 16 < 4, pltpu.roll(mask[h][0], NY - 4 - 4 * f, 1), right)
                left = jnp.where(lane % 16 >= 12, pltpu.roll(mask[h][1], 12 - 4 * f, 1), left)
            ya_ref[f, h] = jnp.where(even, right, left)
            yb_ref[f, h] = jnp.where(even, left, right)
    send_rows(par_ref[0], NZ, q_ref, m_ref, xa_ref, (xb_ref, xb2_ref))


def fetch_kernel(par_ref, w_hbm, ws_hbm, after_ref, w_ref, ws_ref, sems):
    copies = [pltpu.make_async_copy(w_hbm, w_ref, sems.at[0]), pltpu.make_async_copy(ws_hbm, ws_ref, sems.at[1])]
    for copy in copies:
        copy.start()
    for copy in copies:
        copy.wait()


def strip_kernel(par_ref, yb_ref, ya_ref, t_ref, ts_ref, xa_ref, xb_ref):
    even = par_ref[1] == 0
    lane = lanes((NX, NY))
    low = lane % 32 < 16
    place = lane % 16

    def put(h, left, right):
        yield h, jnp.where(low, left, right)
        yield h + 2, jnp.where(low, pltpu.roll(left, NY - 16, 1), pltpu.roll(right, 16, 1))

    for h in range(2):
        mleft = mright = jnp.zeros((NX, NY), F32)
        for f in range(NF):
            a = ya_ref[f, h]
            b = yb_ref[f, h]
            left = jnp.where(even, b, a)
            right = jnp.where(even, a, b)
            if f < 3:
                mleft = jnp.where(place // 4 == f + 1, pltpu.roll(left, 4 + 4 * f, 1), mleft)
                mright = jnp.where(place // 4 == f, pltpu.roll(right, NY - 12 + 4 * f, 1), mright)
            for zi, value in put(h, left, right):
                t_ref[f, zi] = value
        for zi, value in put(h, mleft, mright):
            ts_ref[zi] = value
    send_rows(par_ref[0], 4, t_ref, ts_ref, xa_ref, (xb_ref,))


def update(alpha, beta, center, around, base, solid):
    scale = beta * time_step * 2.0 / 3.0
    nu = beta * viscosity * time_step / 12.0
    u, v, w, p = center
    speed = [-scale * u, -scale * v, -scale * w]
    keep = beta - 90.0 * nu - (beta * time_step * penalty) * solid

    def first(plus, minus, plus2, minus2):
        return (plus - minus) - 0.125 * (plus2 - minus2)

    out = []
    x, z, dy, _ = around(3)
    p_diff = [first(*x), dy, first(*z)]
    divergence = None
    for k in range(3):
        x, z, dy, sy = around(k)
        diffs = [first(*x), dy, first(*z)]
        near = (x[0] + x[1]) + (z[0] + z[1])
        far = (x[2] + x[3]) + (z[2] + z[3])
        total = center[k] * keep - scale * p_diff[k]
        for d in range(3):
            total = total + speed[d] * diffs[d]
        divergence = diffs[k] if divergence is None else divergence + diffs[k]
        total = total + nu * ((16.0 * near - far) + sy)
        if k == 0:
            total = total + beta * time_step * forcing
        out.append(total)
    out.append(beta * p - (sound_sq * scale) * divergence)
    if alpha:
        out = [o + alpha * base(f) for f, o in enumerate(out)]
    return out


def y_weights():
    taps = [(1, 1.0, 16.0), (-1, -1.0, 16.0), (2, -0.125, -1.0), (-2, 0.125, -1.0)]
    wide = np.zeros((4, 512, 256), np.float32)
    strip = np.zeros((1280, 256), np.float32)
    for o, first, second in taps:
        for j in range(NY):
            for zq in range(4):
                c = j + o
                if 0 <= c < NY:
                    rows = (c, c + 128)
                else:
                    lane = 32 * zq + 16 + (c if c < 0 else c - NY)
                    rows = (256 + lane, 384 + lane)
                for r in rows:
                    wide[zq, r, j] = first
                    wide[zq, r, j + NY] = second
            g, place = j // 32, j % 32
            c = place - 16 if place < 16 else NY + place - 16
            left = place < 16
            c += o
            if c < -16 or c >= NY + 16:
                continue
            if (left and c < 0) or (not left and c >= NY):
                lane = 32 * g + 16 + (c if c < 0 else c - NY)
                rows = (lane, lane + 128)
            else:
                rows = (256 + 256 * g + c, 384 + 256 * g + c)
            for r in rows:
                strip[r, j] = first
                strip[r, j + NY] = second
    return jnp.asarray(wide, jnp.bfloat16), jnp.asarray(strip, jnp.bfloat16)


def split(a):
    high = a.astype(jnp.bfloat16)
    return high, (a - high.astype(F32)).astype(jnp.bfloat16)


EARLY = {1: (4, 3, 24), 2: (8, 2, 16)}
FRAME = {1: ((-12, 2), (28, 2)), 2: ((-8, 2), (24, 2)), 3: ((-6, 6),), 4: ((-4, 5),), 5: ((-2, 5),), 6: ((0, 4),)}
WEIGHTS = [(0.0, 1.0), (0.75, 0.25), (1.0 / 3.0, 2.0 / 3.0)]


def ghosts(strip, rows):
    for f in range(NF):
        for zi in range(4):
            strip[f, (zi + 6) % 8, rows, :] = pltpu.roll(strip[f, zi + 2, rows, :], 96 if zi < 2 else 32, 1)


def stage(number, windows, state, w_ref, ws_ref, yd, ytd, out_ref=None):
    q, s1, s2, solid, tq, t1, t2, tsolid = state
    section = (number - 1) % 3
    alpha, beta = WEIGHTS[section]
    cur, tcur = [(q, tq), (s1, t1), (s2, t2)][section]
    out, tout = [(s1, t1), (s2, t2), (q, tq)][section]
    base, tbase = q, tq
    windows = [(OWN + first, count) for first, count in windows]
    tiles = [first + 8 * i for first, count in windows for i in range(count)]
    rows = 8 * len(tiles)
    last = out_ref is not None

    def flat(ref, f, fields, z):
        parts = [ref[pl.ds(f, fields), pl.ds(z, 4), pl.ds(first, 8 * count), :] for first, count in windows]
        return split(jnp.concatenate(parts, axis=2).reshape(4 * fields * rows, NY))

    def along_y(fields, f, carry):
        t = flat(tcur, f, fields, 2)
        every = list(t)
        for zq in range(4):
            a = flat(cur, f, fields, 4 * zq)
            every += a
            y = jnp.dot(jnp.concatenate(a + t, axis=1), w_ref[zq], preferred_element_type=F32)
            yd[pl.ds(f, fields), 4 * zq:4 * zq + 4, 0:rows, :] = y.reshape(fields, 4, rows, 2 * NY)
        if not last:
            y = jnp.dot(jnp.concatenate(every, axis=1), ws_ref[...], preferred_element_type=F32)
            ytd[pl.ds(f, fields), :, 0:rows, :] = y.reshape(fields, 4, rows, 2 * NY)
        return carry

    if rows < 32:
        along_y(NF, 0, 0)
    else:
        lax.fori_loop(0, NF, functools.partial(along_y, 1), 0)

    def strips(half, zi, carry):
        for i, r in enumerate(tiles):
            rr, yr = pl.ds(r, 8), pl.ds(8 * i, 8)

            def around(f):
                x = [tcur[f, zi + 2, pl.ds(r + o, 8), :] for o in (1, -1, 2, -2)]
                z = [tcur[f, zi + 2 + o, rr, :] for o in (1, -1, 2, -2)]
                return x, z, ytd[f, zi, yr, 0:NY], ytd[f, zi, yr, NY:]

            center = [tcur[f, zi + 2, rr, :] for f in range(NF)]
            new = update(alpha, beta, center, around,
                         lambda f: tbase[f, zi + 2, rr, :], tsolid[zi, rr, :])
            for f in range(NF):
                tout[f, zi + 2, rr, :] = new[f]
                tout[f, zi + (6 if half == 0 else -2), rr, :] = pltpu.roll(new[f], 32 if half else 96, 1)
        return carry

    def main(z, carry):
        zs = [lax.rem(z + o, NZ) for o in (1, NZ - 1, 2, NZ - 2)]
        for i, r in enumerate(tiles):
            rr, yr = pl.ds(r, 8), pl.ds(8 * i, 8)

            def around(f):
                x = [cur[f, z, pl.ds(r + o, 8), :] for o in (1, -1, 2, -2)]
                zz = [cur[f, k, rr, :] for k in zs]
                return x, zz, yd[f, z, yr, 0:NY], yd[f, z, yr, NY:]

            center = [cur[f, z, rr, :] for f in range(NF)]
            new = update(alpha, beta, center, around,
                         lambda f: base[f, z, rr, :], solid[z, rr, :])
            for f in range(NF):
                if last:
                    out_ref[f, z, pl.ds(r - OWN, 8), :] = new[f]
                else:
                    out[f, z, rr, :] = new[f]
        return carry

    if not last:
        for half in range(2):
            lax.fori_loop(2 * half, 2 * half + 2, functools.partial(strips, half), 0)
    lax.fori_loop(0, NZ, main, 0)
    return out, tout


def split(a):
    high = a.astype(jnp.bfloat16)
    return high, (a - high.astype(F32)).astype(jnp.bfloat16)


def own_rows(q_in, m_in, t_in, ts_in, state):
    q, s1, s2, solid, tq, t1, t2, tsolid = state
    for f in range(NF):
        q[f, :, OWN:BOTTOM, :] = q_in[f]
        tq[f, 2:6, OWN:BOTTOM, :] = t_in[f]
    solid[:, OWN:BOTTOM, :] = m_in[...].astype(F32)
    tsolid[:, OWN:BOTTOM, :] = ts_in[...]


def early_kernel(par_ref, q_in, m_in, t_in, ts_in, w_ref, ws_ref, *refs):
    results, state, (yd, ytd) = refs[:2 * len(EARLY)], refs[2 * len(EARLY):-2], refs[-2:]
    own_rows(q_in, m_in, t_in, ts_in, state)
    for r in range(OWN, BOTTOM, 8):
        ghosts(state[4], pl.ds(r, 8))
    for number, (first, tiles, _) in EARLY.items():
        out, tout = stage(number, [(first, tiles)], state, w_ref, ws_ref, yd, ytd)
        rows = pl.ds(OWN + first, 8 * tiles)
        for f in range(NF):
            results[2 * number - 2][f] = out[f, :, rows, :]
            results[2 * number - 1][f] = tout[f, 2:6, rows, :]


def main_kernel(par_ref, q_in, m_in, xa_ref, xb_ref, xb2_ref, t_in, ts_in, ca_ref, cb_ref, w_ref, ws_ref, *refs):
    results, out_ref = refs[:2 * len(EARLY)], refs[2 * len(EARLY)]
    state, (yd, ytd) = refs[2 * len(EARLY) + 1:-2], refs[-2:]
    q, s1, s2, solid, tq, t1, t2, tsolid = state
    px = par_ref[0]
    own_rows(q_in, m_in, t_in, ts_in, state)

    def halo(msgs, shift, fields, mask, top):
        row = TOP if top else BOTTOM
        mrow = TOP + 2 if top else BOTTOM
        places = [(msg, i * MSG) for msg in msgs for i in range(msg.shape[0] // MSG)]
        for z, (msg, at) in enumerate(places):
            for f in range(NF):
                fields[f, z + shift, row:row + DEPTH, :] = msg[at + f * DEPTH:at + (f + 1) * DEPTH]
            mask[z, mrow:mrow + DEPTH - 2, :] = msg[at + NF * DEPTH:at + MSG]

    def halos(a_bottom):
        halo((xa_ref,), 0, q, solid, not a_bottom)
        halo((xb_ref, xb2_ref), 0, q, solid, a_bottom)
        halo((ca_ref,), 2, tq, tsolid, not a_bottom)
        halo((cb_ref,), 2, tq, tsolid, a_bottom)

    pl.when(px == 0)(lambda: halos(True))
    pl.when(px == 1)(lambda: halos(False))
    for r in range(0, ROWS, 8):
        ghosts(tq, pl.ds(r, 8))

    for number in range(1, STAGES + 1):
        out, tout = stage(number, FRAME[number], state, w_ref, ws_ref, yd, ytd,
                          out_ref if number == STAGES else None)
        if number in EARLY:
            first, _, valid = EARLY[number]
            rows = pl.ds(OWN + first, valid)
            for f in range(NF):
                out[f, :, rows, :] = results[2 * number - 2][f, :, 0:valid, :]
                tout[f, 2:6, rows, :] = results[2 * number - 1][f, :, 0:valid, :]
            for r in range(0, valid - valid % 8, 8):
                ghosts(tout, pl.ds(OWN + first + r, 8))
            if valid % 8:
                ghosts(tout, pl.ds(OWN + first + valid - 8, 8))


def call(kernel, outs, scratch=(), inputs=0, hbm=0, vmem_mib=32):
    vmem = pl.BlockSpec(memory_space=pltpu.VMEM)
    specs = [pl.BlockSpec(memory_space=pltpu.SMEM)] + [pl.BlockSpec(memory_space=pl.ANY)] * hbm + [vmem] * inputs
    return pl.pallas_call(
        kernel,
        out_shape=[s if isinstance(s, jax.ShapeDtypeStruct) else jax.ShapeDtypeStruct(s, F32) for s in outs],
        in_specs=specs,
        out_specs=[vmem] * len(outs),
        scratch_shapes=list(scratch),
        compiler_params=pltpu.CompilerParams(vmem_limit_bytes=vmem_mib * 2 ** 20),
    )


def solution(mesh):
    nx, ny = mesh.shape["gx"], mesh.shape["gy"]

    def pairs(count, parity):
        return [(i, (i + 1) % count if i % 2 == parity else (i - 1) % count) for i in range(count)]

    def body(fields, solid_mask):
        parity = jnp.stack([lax.axis_index("gx") % 2, lax.axis_index("gy") % 2]).astype(jnp.int32)
        ymsg = (NF, 2, NX, NY)
        parts = [(-(count * MSG) // 8 * -8, NY) for count in (FIRST, NZ - FIRST)]
        own = [jax.ShapeDtypeStruct(a.shape, a.dtype) for a in (fields, solid_mask)]
        yb, ya, xa, xb, xb2, q, m = call(
            pack_kernel, [ymsg, ymsg, (NZ * MSG, NY)] + parts + own, [pltpu.SemaphoreType.DMA((NF + 1,))],
            hbm=2, vmem_mib=32)(parity, fields, solid_mask)
        yb = lax.ppermute(yb, "gy", pairs(ny, 1))
        ya = lax.ppermute(ya, "gy", pairs(ny, 0))
        xb = lax.ppermute(xb, "gx", pairs(nx, 1))
        xb2 = lax.ppermute(xb2, "gx", pairs(nx, 1))
        xa = lax.ppermute(xa, "gx", pairs(nx, 0))
        t, ts, ca, cb = call(strip_kernel, [(NF, 4, NX, NY), (4, NX, NY), (4 * MSG, NY), (4 * MSG, NY)],
                             inputs=2)(parity, yb, ya)
        w = y_weights()
        w = call(fetch_kernel, [jax.ShapeDtypeStruct(a.shape, a.dtype) for a in w],
                 [pltpu.SemaphoreType.DMA((2,))], hbm=3)(parity, *w, cb)
        cb = lax.ppermute(cb, "gx", pairs(nx, 1))
        ca = lax.ppermute(ca, "gx", pairs(nx, 0))
        wide = (NF, NZ, ROWS, NY)
        narrow = (NF, 8, ROWS, NY)
        scratch = [wide] * 3 + [(NZ, ROWS, NY)] + [narrow] * 3 + [(4, ROWS, NY)]
        scratch += [(NF, NZ, 48, 2 * NY), (NF, 4, 48, 2 * NY)]
        scratch = [pltpu.VMEM(s, F32) for s in scratch]
        parts = []
        for _, tiles, _ in EARLY.values():
            parts += [(NF, NZ, 8 * tiles, NY), (NF, 4, 8 * tiles, NY)]
        early = call(early_kernel, parts, scratch, inputs=6, vmem_mib=32)(parity, q, m, t, ts, *w)
        out, = call(main_kernel, [(NF, NZ, NX, NY)], scratch, inputs=11 + len(parts), vmem_mib=32)(
            parity, q, m, xa, xb, xb2, t, ts, ca, cb, *w, *early)
        return out

    return jax.shard_map(
        body,
        mesh=mesh,
        in_specs=(P(None, None, "gx", "gy"), P(None, "gx", "gy")),
        out_specs=P(None, None, "gx", "gy"),
        check_vma=False,
    )
```

```python
import functools

import jax
import jax.numpy as jnp
import numpy as np
from jax import lax
from jax.sharding import PartitionSpec as P
from jax.experimental import pallas as pl
from jax.experimental.pallas import tpu as pltpu

STAGES = 6
DEPTH = 2 * STAGES
viscosity = 0.05
penalty = 10.0
forcing = 0.5
sound_sq = 2.25
time_step = 0.2

NF, NZ, NX, NY = 4, 16, 32, 128
ROWS = 64
OWN = 16
TOP = OWN - DEPTH
BOTTOM = OWN + NX
MSG = (NF + 1) * DEPTH - 2
F32 = jnp.float32
LAYERS = 4
FIRST = 8


def lanes(shape):
    return lax.broadcasted_iota(jnp.int32, shape, len(shape) - 1)


def send_rows(px, layers, q_ref, m_ref, a_ref, b_refs):
    def put(dst, bottom, first, count):
        start = NX - DEPTH if bottom else 0
        mstart = NX - DEPTH + 2 if bottom else 0
        for z in range(count):
            for f in range(NF):
                dst[z * MSG + f * DEPTH:z * MSG + (f + 1) * DEPTH] = q_ref[f, first + z, start:start + DEPTH, :]
            dst[z * MSG + NF * DEPTH:(z + 1) * MSG] = m_ref[first + z, mstart:mstart + DEPTH - 2, :]

    def send(a_bottom):
        put(a_ref, a_bottom, 0, layers)
        first = 0
        for b_ref in b_refs:
            count = b_ref.shape[0] // MSG
            put(b_ref, not a_bottom, first, count)
            first += count

    pl.when(px == 0)(lambda: send(True))
    pl.when(px == 1)(lambda: send(False))


def pack_kernel(par_ref, q_ref, m_ref, yb_ref, ya_ref, xa_ref, xb_ref, xb2_ref):
    lane = lanes((NX, NY))
    group = lane // 32
    low = lane % 32 < 16
    even = par_ref[1] == 0

    def packed(load, zi):
        out = pltpu.roll(load(zi), 16, 1)
        for zq in range(1, 4):
            out = jnp.where(group == zq, pltpu.roll(load(4 * zq + zi), (16 + 32 * zq) % NY, 1), out)
        return out

    def both(load, h):
        first, second = packed(load, h), packed(load, h + 2)
        return (jnp.where(low, first, pltpu.roll(second, 16, 1)),
                jnp.where(low, pltpu.roll(second, NY - 16, 1), first))

    mask = [both(lambda z: m_ref[z], h) for h in range(2)]
    for f in range(NF):
        for h in range(2):
            right, left = both(lambda z: q_ref[f, z], h)
            if f < 3:
                right = jnp.where(lane % 16 < 4, pltpu.roll(mask[h][0], NY - 4 - 4 * f, 1), right)
                left = jnp.where(lane % 16 >= 12, pltpu.roll(mask[h][1], 12 - 4 * f, 1), left)
            ya_ref[f, h] = jnp.where(even, right, left)
            yb_ref[f, h] = jnp.where(even, left, right)
    send_rows(par_ref[0], NZ, q_ref, m_ref, xa_ref, (xb_ref, xb2_ref))


def fetch_kernel(par_ref, w_hbm, ws_hbm, after_ref, w_ref, ws_ref, sems):
    copies = [pltpu.make_async_copy(w_hbm, w_ref, sems.at[0]), pltpu.make_async_copy(ws_hbm, ws_ref, sems.at[1])]
    for copy in copies:
        copy.start()
    for copy in copies:
        copy.wait()


def strip_kernel(par_ref, yb_ref, ya_ref, t_ref, ts_ref, xa_ref, xb_ref):
    even = par_ref[1] == 0
    lane = lanes((NX, NY))
    low = lane % 32 < 16
    place = lane % 16

    def put(h, left, right):
        yield h, jnp.where(low, left, right)
        yield h + 2, jnp.where(low, pltpu.roll(left, NY - 16, 1), pltpu.roll(right, 16, 1))

    for h in range(2):
        mleft = mright = jnp.zeros((NX, NY), F32)
        for f in range(NF):
            a = ya_ref[f, h]
            b = yb_ref[f, h]
            left = jnp.where(even, b, a)
            right = jnp.where(even, a, b)
            if f < 3:
                mleft = jnp.where(place // 4 == f + 1, pltpu.roll(left, 4 + 4 * f, 1), mleft)
                mright = jnp.where(place // 4 == f, pltpu.roll(right, NY - 12 + 4 * f, 1), mright)
            for zi, value in put(h, left, right):
                t_ref[f, zi] = value
        for zi, value in put(h, mleft, mright):
            ts_ref[zi] = value
    send_rows(par_ref[0], 4, t_ref, ts_ref, xa_ref, (xb_ref,))


def update(alpha, beta, center, around, base, solid):
    scale = beta * time_step * 2.0 / 3.0
    nu = beta * viscosity * time_step / 12.0
    u, v, w, p = center
    speed = [-scale * u, -scale * v, -scale * w]
    keep = beta - 90.0 * nu - (beta * time_step * penalty) * solid

    def first(plus, minus, plus2, minus2):
        return (plus - minus) - 0.125 * (plus2 - minus2)

    out = []
    x, z, dy, _ = around(3)
    p_diff = [first(*x), dy, first(*z)]
    divergence = None
    for k in range(3):
        x, z, dy, sy = around(k)
        diffs = [first(*x), dy, first(*z)]
        near = (x[0] + x[1]) + (z[0] + z[1])
        far = (x[2] + x[3]) + (z[2] + z[3])
        total = center[k] * keep - scale * p_diff[k]
        for d in range(3):
            total = total + speed[d] * diffs[d]
        divergence = diffs[k] if divergence is None else divergence + diffs[k]
        total = total + nu * ((16.0 * near - far) + sy)
        if k == 0:
            total = total + beta * time_step * forcing
        out.append(total)
    out.append(beta * p - (sound_sq * scale) * divergence)
    if alpha:
        out = [o + alpha * base(f) for f, o in enumerate(out)]
    return out


def y_weights():
    taps = [(1, 1.0, 16.0), (-1, -1.0, 16.0), (2, -0.125, -1.0), (-2, 0.125, -1.0)]
    wide = np.zeros((4, 512, 256), np.float32)
    strip = np.zeros((1280, 256), np.float32)
    for o, first, second in taps:
        for j in range(NY):
            for zq in range(4):
                c = j + o
                if 0 <= c < NY:
                    rows = (c, c + 128)
                else:
                    lane = 32 * zq + 16 + (c if c < 0 else c - NY)
                    rows = (256 + lane, 384 + lane)
                for r in rows:
                    wide[zq, r, j] = first
                    wide[zq, r, j + NY] = second
            g, place = j // 32, j % 32
            c = place - 16 if place < 16 else NY + place - 16
            left = place < 16
            c += o
            if c < -16 or c >= NY + 16:
                continue
            if (left and c < 0) or (not left and c >= NY):
                lane = 32 * g + 16 + (c if c < 0 else c - NY)
                rows = (lane, lane + 128)
            else:
                rows = (256 + 256 * g + c, 384 + 256 * g + c)
            for r in rows:
                strip[r, j] = first
                strip[r, j + NY] = second
    return jnp.asarray(wide, jnp.bfloat16), jnp.asarray(strip, jnp.bfloat16)


def split(a):
    high = a.astype(jnp.bfloat16)
    return high, (a - high.astype(F32)).astype(jnp.bfloat16)


EARLY = {1: (4, 3, 24), 2: (8, 2, 16)}
FRAME = {1: ((-12, 2), (28, 2)), 2: ((-8, 2), (24, 2)), 3: ((-6, 6),), 4: ((-4, 5),), 5: ((-2, 5),), 6: ((0, 4),)}
WEIGHTS = [(0.0, 1.0), (0.75, 0.25), (1.0 / 3.0, 2.0 / 3.0)]


def ghosts(strip, rows):
    for f in range(NF):
        for zi in range(4):
            strip[f, (zi + 6) % 8, rows, :] = pltpu.roll(strip[f, zi + 2, rows, :], 96 if zi < 2 else 32, 1)


def stage(number, windows, state, w_ref, ws_ref, yd, ytd, out_ref=None):
    q, s1, s2, solid, tq, t1, t2, tsolid = state
    section = (number - 1) % 3
    alpha, beta = WEIGHTS[section]
    cur, tcur = [(q, tq), (s1, t1), (s2, t2)][section]
    out, tout = [(s1, t1), (s2, t2), (q, tq)][section]
    base, tbase = q, tq
    windows = [(OWN + first, count) for first, count in windows]
    tiles = [first + 8 * i for first, count in windows for i in range(count)]
    rows = 8 * len(tiles)
    last = out_ref is not None

    def flat(ref, f, fields, z):
        parts = [ref[pl.ds(f, fields), pl.ds(z, 4), pl.ds(first, 8 * count), :] for first, count in windows]
        return split(jnp.concatenate(parts, axis=2).reshape(4 * fields * rows, NY))

    def along_y(fields, f, carry, width=2 * NY):
        t = flat(tcur, f, fields, 2)
        every = list(t)
        for zq in range(4):
            a = flat(cur, f, fields, 4 * zq)
            every += a
            y = jnp.dot(jnp.concatenate(a + t, axis=1), w_ref[zq, :, 0:width], preferred_element_type=F32)
            yd[pl.ds(f, fields), 4 * zq:4 * zq + 4, 0:rows, 0:width] = y.reshape(fields, 4, rows, width)
        if not last:
            y = jnp.dot(jnp.concatenate(every, axis=1), ws_ref[:, 0:width], preferred_element_type=F32)
            ytd[pl.ds(f, fields), :, 0:rows, 0:width] = y.reshape(fields, 4, rows, width)
        return carry

    if rows < 32:
        along_y(NF, 0, 0)
    else:
        lax.fori_loop(0, 3, functools.partial(along_y, 1), 0)
        along_y(1, 3, 0, NY)

    def strips(half):
        zi = 2 * half
        here = slice(zi + 2, zi + 4)
        for i, r in enumerate(tiles):
            rr, yr = pl.ds(r, 8), pl.ds(8 * i, 8)

            def around(f):
                planes = [tcur[f, zi + k, rr, :] for k in range(6)]
                x = [tcur[f, here, pl.ds(r + o, 8), :] for o in (1, -1, 2, -2)]
                z = [jnp.stack(planes[2 + o:4 + o]) for o in (1, -1, 2, -2)]
                return x, z, ytd[f, zi:zi + 2, yr, 0:NY], ytd[f, zi:zi + 2, yr, NY:]

            center = [tcur[f, here, rr, :] for f in range(NF)]
            new = update(alpha, beta, center, around,
                         lambda f: tbase[f, here, rr, :], tsolid[zi:zi + 2, rr, :])
            for f in range(NF):
                tout[f, here, rr, :] = new[f]
                for k in range(2):
                    tout[f, zi + k + (6 if half == 0 else -2), rr, :] = pltpu.roll(new[f][k], 32 if half else 96, 1)

    def main(step, carry):
        z = LAYERS * step
        here = pl.ds(z, LAYERS)
        zs = [lax.rem(z + NZ + o, NZ) for o in range(-2, LAYERS + 2)]
        for i, r in enumerate(tiles):
            rr, yr = pl.ds(r, 8), pl.ds(8 * i, 8)
            def around(f):
                planes = [cur[f, k, rr, :] for k in zs]
                x = [cur[f, here, pl.ds(r + o, 8), :] for o in (1, -1, 2, -2)]
                zz = [jnp.stack(planes[2 + o:2 + o + LAYERS]) for o in (1, -1, 2, -2)]
                return x, zz, yd[f, here, yr, 0:NY], yd[f, here, yr, NY:]

            center = [cur[f, here, rr, :] for f in range(NF)]
            new = update(alpha, beta, center, around,
                         lambda f: base[f, here, rr, :], solid[here, rr, :])
            for f in range(NF):
                if last:
                    out_ref[f, here, pl.ds(r - OWN, 8), :] = new[f]
                else:
                    out[f, here, rr, :] = new[f]
        return carry

    if not last:
        for half in range(2):
            strips(half)
    lax.fori_loop(0, NZ // LAYERS, main, 0)
    return out, tout


def split(a):
    high = a.astype(jnp.bfloat16)
    return high, (a - high.astype(F32)).astype(jnp.bfloat16)


def own_rows(q_in, m_in, t_in, ts_in, state):
    q, s1, s2, solid, tq, t1, t2, tsolid = state
    for f in range(NF):
        q[f, :, OWN:BOTTOM, :] = q_in[f]
        tq[f, 2:6, OWN:BOTTOM, :] = t_in[f]
    solid[:, OWN:BOTTOM, :] = m_in[...]
    tsolid[:, OWN:BOTTOM, :] = ts_in[...]


def early_kernel(par_ref, q_in, m_in, t_in, ts_in, w_ref, ws_ref, *refs):
    results, state, (yd, ytd) = refs[:2 * len(EARLY)], refs[2 * len(EARLY):-2], refs[-2:]
    own_rows(q_in, m_in, t_in, ts_in, state)
    for r in range(OWN, BOTTOM, 8):
        ghosts(state[4], pl.ds(r, 8))
    for number, (first, tiles, _) in EARLY.items():
        out, tout = stage(number, [(first, tiles)], state, w_ref, ws_ref, yd, ytd)
        rows = pl.ds(OWN + first, 8 * tiles)
        for f in range(NF):
            results[2 * number - 2][f] = out[f, :, rows, :]
            results[2 * number - 1][f] = tout[f, 2:6, rows, :]


def main_kernel(par_ref, q_in, m_in, xa_ref, xb_ref, xb2_ref, t_in, ts_in, ca_ref, cb_ref, w_ref, ws_ref, *refs):
    results, out_ref = refs[:2 * len(EARLY)], refs[2 * len(EARLY)]
    state, (yd, ytd) = refs[2 * len(EARLY) + 1:-2], refs[-2:]
    q, s1, s2, solid, tq, t1, t2, tsolid = state
    px = par_ref[0]
    own_rows(q_in, m_in, t_in, ts_in, state)

    def halo(msgs, shift, fields, mask, top):
        row = TOP if top else BOTTOM
        mrow = TOP + 2 if top else BOTTOM
        places = [(msg, i * MSG) for msg in msgs for i in range(msg.shape[0] // MSG)]
        for z, (msg, at) in enumerate(places):
            for f in range(NF):
                fields[f, z + shift, row:row + DEPTH, :] = msg[at + f * DEPTH:at + (f + 1) * DEPTH]
            mask[z, mrow:mrow + DEPTH - 2, :] = msg[at + NF * DEPTH:at + MSG]

    def halos(a_bottom):
        halo((xa_ref,), 0, q, solid, not a_bottom)
        halo((xb_ref, xb2_ref), 0, q, solid, a_bottom)
        halo((ca_ref,), 2, tq, tsolid, not a_bottom)
        halo((cb_ref,), 2, tq, tsolid, a_bottom)

    pl.when(px == 0)(lambda: halos(True))
    pl.when(px == 1)(lambda: halos(False))
    for r in range(0, ROWS, 8):
        ghosts(tq, pl.ds(r, 8))

    for number in range(1, STAGES + 1):
        out, tout = stage(number, FRAME[number], state, w_ref, ws_ref, yd, ytd,
                          out_ref if number == STAGES else None)
        if number in EARLY:
            first, _, valid = EARLY[number]
            rows = pl.ds(OWN + first, valid)
            for f in range(NF):
                out[f, :, rows, :] = results[2 * number - 2][f, :, 0:valid, :]
                tout[f, 2:6, rows, :] = results[2 * number - 1][f, :, 0:valid, :]
            for r in range(0, valid - valid % 8, 8):
                ghosts(tout, pl.ds(OWN + first + r, 8))
            if valid % 8:
                ghosts(tout, pl.ds(OWN + first + valid - 8, 8))


def call(kernel, outs, scratch=(), inputs=0, hbm=0, vmem_mib=32):
    vmem = pl.BlockSpec(memory_space=pltpu.VMEM)
    specs = [pl.BlockSpec(memory_space=pltpu.SMEM)] + [pl.BlockSpec(memory_space=pl.ANY)] * hbm + [vmem] * inputs
    return pl.pallas_call(
        kernel,
        out_shape=[s if isinstance(s, jax.ShapeDtypeStruct) else jax.ShapeDtypeStruct(s, F32) for s in outs],
        in_specs=specs,
        out_specs=[vmem] * len(outs),
        scratch_shapes=list(scratch),
        compiler_params=pltpu.CompilerParams(vmem_limit_bytes=vmem_mib * 2 ** 20),
    )


def solution(mesh):
    nx, ny = mesh.shape["gx"], mesh.shape["gy"]

    def pairs(count, parity):
        return [(i, (i + 1) % count if i % 2 == parity else (i - 1) % count) for i in range(count)]

    def body(fields, solid_mask):
        parity = jnp.stack([lax.axis_index("gx") % 2, lax.axis_index("gy") % 2]).astype(jnp.int32)
        ymsg = (NF, 2, NX, NY)
        parts = [(-(count * MSG) // 8 * -8, NY) for count in (FIRST, NZ - FIRST)]
        q, m = fields, solid_mask.astype(F32)
        yb, ya, xa, xb, xb2 = call(pack_kernel, [ymsg, ymsg, (NZ * MSG, NY)] + parts, inputs=2)(parity, q, m)
        yb = lax.ppermute(yb, "gy", pairs(ny, 1))
        ya = lax.ppermute(ya, "gy", pairs(ny, 0))
        xb = lax.ppermute(xb, "gx", pairs(nx, 1))
        xb2 = lax.ppermute(xb2, "gx", pairs(nx, 1))
        xa = lax.ppermute(xa, "gx", pairs(nx, 0))
        t, ts, ca, cb = call(strip_kernel, [(NF, 4, NX, NY), (4, NX, NY), (4 * MSG, NY), (4 * MSG, NY)],
                             inputs=2)(parity, yb, ya)
        w = y_weights()
        w = call(fetch_kernel, [jax.ShapeDtypeStruct(a.shape, a.dtype) for a in w],
                 [pltpu.SemaphoreType.DMA((2,))], hbm=3)(parity, *w, cb)
        cb = lax.ppermute(cb, "gx", pairs(nx, 1))
        ca = lax.ppermute(ca, "gx", pairs(nx, 0))
        wide = (NF, NZ, ROWS, NY)
        narrow = (NF, 8, ROWS, NY)
        scratch = [wide] * 3 + [(NZ, ROWS, NY)] + [narrow] * 3 + [(4, ROWS, NY)]
        scratch += [(NF, NZ, 48, 2 * NY), (NF, 4, 48, 2 * NY)]
        scratch = [pltpu.VMEM(s, F32) for s in scratch]
        parts = []
        for _, tiles, _ in EARLY.values():
            parts += [(NF, NZ, 8 * tiles, NY), (NF, 4, 8 * tiles, NY)]
        early = call(early_kernel, parts, scratch, inputs=6, vmem_mib=32)(parity, q, m, t, ts, *w)
        out, = call(main_kernel, [(NF, NZ, NX, NY)], scratch, inputs=11 + len(parts), vmem_mib=32)(
            parity, q, m, xa, xb, xb2, t, ts, ca, cb, *w, *early)
        return out

    return jax.shard_map(
        body,
        mesh=mesh,
        in_specs=(P(None, None, "gx", "gy"), P(None, "gx", "gy")),
        out_specs=P(None, None, "gx", "gy"),
        check_vma=False,
    )
```

```python
import functools

import jax
import jax.numpy as jnp
import numpy as np
from jax import lax
from jax.sharding import PartitionSpec as P
from jax.experimental import pallas as pl
from jax.experimental.pallas import tpu as pltpu

STAGES = 6
DEPTH = 2 * STAGES
viscosity = 0.05
penalty = 10.0
forcing = 0.5
sound_sq = 2.25
time_step = 0.2

NF, NZ, NX, NY = 4, 16, 32, 128
ROWS = 64
OWN = 16
TOP = OWN - DEPTH
BOTTOM = OWN + NX
MSG = (NF + 1) * DEPTH - 2
F32 = jnp.float32
LAYERS = 4
FIRST = 8


def lanes(shape):
    return lax.broadcasted_iota(jnp.int32, shape, len(shape) - 1)


def send_rows(px, layers, q_ref, m_ref, a_ref, b_refs):
    def put(dst, bottom, first, count):
        start = NX - DEPTH if bottom else 0
        mstart = NX - DEPTH + 2 if bottom else 0
        for z in range(count):
            for f in range(NF):
                dst[z * MSG + f * DEPTH:z * MSG + (f + 1) * DEPTH] = q_ref[f, first + z, start:start + DEPTH, :]
            dst[z * MSG + NF * DEPTH:(z + 1) * MSG] = m_ref[first + z, mstart:mstart + DEPTH - 2, :]

    def send(a_bottom):
        put(a_ref, a_bottom, 0, layers)
        first = 0
        for b_ref in b_refs:
            count = b_ref.shape[0] // MSG
            put(b_ref, not a_bottom, first, count)
            first += count

    pl.when(px == 0)(lambda: send(True))
    pl.when(px == 1)(lambda: send(False))


def pack_kernel(par_ref, q_ref, m_ref, yb_ref, ya_ref, xa_ref, xb_ref, xb2_ref):
    lane = lanes((NX, NY))
    group = lane // 32
    low = lane % 32 < 16
    even = par_ref[1] == 0

    def packed(load, zi):
        out = pltpu.roll(load(zi), 16, 1)
        for zq in range(1, 4):
            out = jnp.where(group == zq, pltpu.roll(load(4 * zq + zi), (16 + 32 * zq) % NY, 1), out)
        return out

    def both(load, h):
        first, second = packed(load, h), packed(load, h + 2)
        return (jnp.where(low, first, pltpu.roll(second, 16, 1)),
                jnp.where(low, pltpu.roll(second, NY - 16, 1), first))

    mask = [both(lambda z: m_ref[z], h) for h in range(2)]
    for f in range(NF):
        for h in range(2):
            right, left = both(lambda z: q_ref[f, z], h)
            if f < 3:
                right = jnp.where(lane % 16 < 4, pltpu.roll(mask[h][0], NY - 4 - 4 * f, 1), right)
                left = jnp.where(lane % 16 >= 12, pltpu.roll(mask[h][1], 12 - 4 * f, 1), left)
            ya_ref[f, h] = jnp.where(even, right, left)
            yb_ref[f, h] = jnp.where(even, left, right)
    send_rows(par_ref[0], NZ, q_ref, m_ref, xa_ref, (xb_ref, xb2_ref))


def fetch_kernel(par_ref, w_hbm, ws_hbm, after_ref, w_ref, ws_ref, sems):
    copies = [pltpu.make_async_copy(w_hbm, w_ref, sems.at[0]), pltpu.make_async_copy(ws_hbm, ws_ref, sems.at[1])]
    for copy in copies:
        copy.start()
    for copy in copies:
        copy.wait()


def strip_kernel(par_ref, yb_ref, ya_ref, t_ref, ts_ref, xa_ref, xb_ref):
    even = par_ref[1] == 0
    lane = lanes((NX, NY))
    low = lane % 32 < 16
    place = lane % 16

    def put(h, left, right):
        yield h, jnp.where(low, left, right)
        yield h + 2, jnp.where(low, pltpu.roll(left, NY - 16, 1), pltpu.roll(right, 16, 1))

    for h in range(2):
        mleft = mright = jnp.zeros((NX, NY), F32)
        for f in range(NF):
            a = ya_ref[f, h]
            b = yb_ref[f, h]
            left = jnp.where(even, b, a)
            right = jnp.where(even, a, b)
            if f < 3:
                mleft = jnp.where(place // 4 == f + 1, pltpu.roll(left, 4 + 4 * f, 1), mleft)
                mright = jnp.where(place // 4 == f, pltpu.roll(right, NY - 12 + 4 * f, 1), mright)
            for zi, value in put(h, left, right):
                t_ref[f, zi] = value
        for zi, value in put(h, mleft, mright):
            ts_ref[zi] = value
    send_rows(par_ref[0], 4, t_ref, ts_ref, xa_ref, (xb_ref,))


def update(alpha, beta, center, around, base, solid):
    scale = beta * time_step * 2.0 / 3.0
    nu = beta * viscosity * time_step / 12.0
    u, v, w, p = center
    speed = [-scale * u, -scale * v, -scale * w]
    keep = beta - 90.0 * nu - (beta * time_step * penalty) * solid

    def first(plus, minus, plus2, minus2):
        return (plus - minus) - 0.125 * (plus2 - minus2)

    out = []
    x, z, dy, _ = around(3)
    p_diff = [first(*x), dy, first(*z)]
    divergence = None
    for k in range(3):
        x, z, dy, sy = around(k)
        diffs = [first(*x), dy, first(*z)]
        near = (x[0] + x[1]) + (z[0] + z[1])
        far = (x[2] + x[3]) + (z[2] + z[3])
        total = center[k] * keep - scale * p_diff[k]
        for d in range(3):
            total = total + speed[d] * diffs[d]
        divergence = diffs[k] if divergence is None else divergence + diffs[k]
        total = total + nu * ((16.0 * near - far) + sy)
        if k == 0:
            total = total + beta * time_step * forcing
        out.append(total)
    out.append(beta * p - (sound_sq * scale) * divergence)
    if alpha:
        out = [o + alpha * base(f) for f, o in enumerate(out)]
    return out


def y_weights():
    taps = [(1, 1.0, 16.0), (-1, -1.0, 16.0), (2, -0.125, -1.0), (-2, 0.125, -1.0)]
    wide = np.zeros((4, 512, 256), np.float32)
    strip = np.zeros((1280, 256), np.float32)
    for o, first, second in taps:
        for j in range(NY):
            for zq in range(4):
                c = j + o
                if 0 <= c < NY:
                    rows = (c, c + 128)
                else:
                    lane = 32 * zq + 16 + (c if c < 0 else c - NY)
                    rows = (256 + lane, 384 + lane)
                for r in rows:
                    wide[zq, r, j] = first
                    wide[zq, r, j + NY] = second
            g, place = j // 32, j % 32
            c = place - 16 if place < 16 else NY + place - 16
            left = place < 16
            c += o
            if c < -16 or c >= NY + 16:
                continue
            if (left and c < 0) or (not left and c >= NY):
                lane = 32 * g + 16 + (c if c < 0 else c - NY)
                rows = (lane, lane + 128)
            else:
                rows = (256 + 256 * g + c, 384 + 256 * g + c)
            for r in rows:
                strip[r, j] = first
                strip[r, j + NY] = second
    return jnp.asarray(wide, jnp.bfloat16), jnp.asarray(strip, jnp.bfloat16)


def split(a):
    high = a.astype(jnp.bfloat16)
    return high, (a - high.astype(F32)).astype(jnp.bfloat16)


EARLY = {1: (2, 4, 28), 2: (4, 3, 24), 3: (8, 2, 16)}
FRAME = {1: ((-10, 2), (26, 2)), 2: ((-8, 2), (24, 2)), 3: ((-6, 2), (22, 2)),
         4: ((-4, 5),), 5: ((-2, 5),), 6: ((0, 4),)}
WEIGHTS = [(0.0, 1.0), (0.75, 0.25), (1.0 / 3.0, 2.0 / 3.0)]


def ghosts(strip, rows):
    for f in range(NF):
        for zi in range(4):
            strip[f, (zi + 6) % 8, rows, :] = pltpu.roll(strip[f, zi + 2, rows, :], 96 if zi < 2 else 32, 1)


def stage(number, windows, state, w_ref, ws_ref, yd, ytd, out_ref=None):
    q, s1, s2, solid, tq, t1, t2, tsolid = state
    section = (number - 1) % 3
    alpha, beta = WEIGHTS[section]
    cur, tcur = [(q, tq), (s1, t1), (s2, t2)][section]
    out, tout = [(s1, t1), (s2, t2), (q, tq)][section]
    base, tbase = q, tq
    windows = [(OWN + first, count) for first, count in windows]
    tiles = [first + 8 * i for first, count in windows for i in range(count)]
    rows = 8 * len(tiles)
    last = out_ref is not None

    def flat(ref, f, fields, z):
        parts = [ref[pl.ds(f, fields), pl.ds(z, 4), pl.ds(first, 8 * count), :] for first, count in windows]
        return split(jnp.concatenate(parts, axis=2).reshape(4 * fields * rows, NY))

    def along_y(fields, f, carry, width=2 * NY):
        t = flat(tcur, f, fields, 2)
        every = list(t)
        for zq in range(4):
            a = flat(cur, f, fields, 4 * zq)
            every += a
            y = jnp.dot(jnp.concatenate(a + t, axis=1), w_ref[zq, :, 0:width], preferred_element_type=F32)
            yd[pl.ds(f, fields), 4 * zq:4 * zq + 4, 0:rows, 0:width] = y.reshape(fields, 4, rows, width)
        if not last:
            y = jnp.dot(jnp.concatenate(every, axis=1), ws_ref[:, 0:width], preferred_element_type=F32)
            ytd[pl.ds(f, fields), :, 0:rows, 0:width] = y.reshape(fields, 4, rows, width)
        return carry

    if rows < 32:
        along_y(NF, 0, 0)
    else:
        lax.fori_loop(0, 3, functools.partial(along_y, 1), 0)
        along_y(1, 3, 0, NY)

    def strips(half):
        zi = 2 * half
        here = slice(zi + 2, zi + 4)
        for i, r in enumerate(tiles):
            rr, yr = pl.ds(r, 8), pl.ds(8 * i, 8)

            def around(f):
                planes = [tcur[f, zi + k, rr, :] for k in range(6)]
                x = [tcur[f, here, pl.ds(r + o, 8), :] for o in (1, -1, 2, -2)]
                z = [jnp.stack(planes[2 + o:4 + o]) for o in (1, -1, 2, -2)]
                return x, z, ytd[f, zi:zi + 2, yr, 0:NY], ytd[f, zi:zi + 2, yr, NY:]

            center = [tcur[f, here, rr, :] for f in range(NF)]
            new = update(alpha, beta, center, around,
                         lambda f: tbase[f, here, rr, :], tsolid[zi:zi + 2, rr, :])
            for f in range(NF):
                tout[f, here, rr, :] = new[f]
                for k in range(2):
                    tout[f, zi + k + (6 if half == 0 else -2), rr, :] = pltpu.roll(new[f][k], 32 if half else 96, 1)

    def main(step, carry):
        z = LAYERS * step
        here = pl.ds(z, LAYERS)
        zs = [lax.rem(z + NZ + o, NZ) for o in range(-2, LAYERS + 2)]
        for i, r in enumerate(tiles):
            rr, yr = pl.ds(r, 8), pl.ds(8 * i, 8)
            def around(f):
                planes = [cur[f, k, rr, :] for k in zs]
                x = [cur[f, here, pl.ds(r + o, 8), :] for o in (1, -1, 2, -2)]
                zz = [jnp.stack(planes[2 + o:2 + o + LAYERS]) for o in (1, -1, 2, -2)]
                return x, zz, yd[f, here, yr, 0:NY], yd[f, here, yr, NY:]

            center = [cur[f, here, rr, :] for f in range(NF)]
            new = update(alpha, beta, center, around,
                         lambda f: base[f, here, rr, :], solid[here, rr, :])
            for f in range(NF):
                if last:
                    out_ref[f, here, pl.ds(r - OWN, 8), :] = new[f]
                else:
                    out[f, here, rr, :] = new[f]
        return carry

    if not last:
        for half in range(2):
            strips(half)
    lax.fori_loop(0, NZ // LAYERS, main, 0)
    return out, tout


def split(a):
    high = a.astype(jnp.bfloat16)
    return high, (a - high.astype(F32)).astype(jnp.bfloat16)


def own_rows(q_in, m_in, t_in, ts_in, state):
    q, s1, s2, solid, tq, t1, t2, tsolid = state
    for f in range(NF):
        q[f, :, OWN:BOTTOM, :] = q_in[f]
        tq[f, 2:6, OWN:BOTTOM, :] = t_in[f]
    solid[:, OWN:BOTTOM, :] = m_in[...]
    tsolid[:, OWN:BOTTOM, :] = ts_in[...]


def early_kernel(par_ref, q_in, m_in, t_in, ts_in, w_ref, ws_ref, *refs):
    results, state, (yd, ytd) = refs[:2 * len(EARLY)], refs[2 * len(EARLY):-2], refs[-2:]
    own_rows(q_in, m_in, t_in, ts_in, state)
    for r in range(OWN, BOTTOM, 8):
        ghosts(state[4], pl.ds(r, 8))
    for number, (first, tiles, _) in EARLY.items():
        out, tout = stage(number, [(first, tiles)], state, w_ref, ws_ref, yd, ytd)
        rows = pl.ds(OWN + first, 8 * tiles)
        for f in range(NF):
            results[2 * number - 2][f] = out[f, :, rows, :]
            results[2 * number - 1][f] = tout[f, 2:6, rows, :]


def main_kernel(par_ref, q_in, m_in, xa_ref, xb_ref, xb2_ref, t_in, ts_in, ca_ref, cb_ref, w_ref, ws_ref, *refs):
    results, out_ref = refs[:2 * len(EARLY)], refs[2 * len(EARLY)]
    state, (yd, ytd) = refs[2 * len(EARLY) + 1:-2], refs[-2:]
    q, s1, s2, solid, tq, t1, t2, tsolid = state
    px = par_ref[0]
    own_rows(q_in, m_in, t_in, ts_in, state)

    def halo(msgs, shift, fields, mask, top):
        row = TOP if top else BOTTOM
        mrow = TOP + 2 if top else BOTTOM
        places = [(msg, i * MSG) for msg in msgs for i in range(msg.shape[0] // MSG)]
        for z, (msg, at) in enumerate(places):
            for f in range(NF):
                fields[f, z + shift, row:row + DEPTH, :] = msg[at + f * DEPTH:at + (f + 1) * DEPTH]
            mask[z, mrow:mrow + DEPTH - 2, :] = msg[at + NF * DEPTH:at + MSG]

    def halos(a_bottom):
        halo((xa_ref,), 0, q, solid, not a_bottom)
        halo((xb_ref, xb2_ref), 0, q, solid, a_bottom)
        halo((ca_ref,), 2, tq, tsolid, not a_bottom)
        halo((cb_ref,), 2, tq, tsolid, a_bottom)

    pl.when(px == 0)(lambda: halos(True))
    pl.when(px == 1)(lambda: halos(False))
    for r in range(0, ROWS, 8):
        ghosts(tq, pl.ds(r, 8))

    for number in range(1, STAGES + 1):
        out, tout = stage(number, FRAME[number], state, w_ref, ws_ref, yd, ytd,
                          out_ref if number == STAGES else None)
        if number in EARLY:
            first, _, valid = EARLY[number]
            rows = pl.ds(OWN + first, valid)
            for f in range(NF):
                out[f, :, rows, :] = results[2 * number - 2][f, :, 0:valid, :]
                tout[f, 2:6, rows, :] = results[2 * number - 1][f, :, 0:valid, :]
            for r in range(0, valid - valid % 8, 8):
                ghosts(tout, pl.ds(OWN + first + r, 8))
            if valid % 8:
                ghosts(tout, pl.ds(OWN + first + valid - 8, 8))


def call(kernel, outs, scratch=(), inputs=0, hbm=0, vmem_mib=32):
    vmem = pl.BlockSpec(memory_space=pltpu.VMEM)
    specs = [pl.BlockSpec(memory_space=pltpu.SMEM)] + [pl.BlockSpec(memory_space=pl.ANY)] * hbm + [vmem] * inputs
    return pl.pallas_call(
        kernel,
        out_shape=[s if isinstance(s, jax.ShapeDtypeStruct) else jax.ShapeDtypeStruct(s, F32) for s in outs],
        in_specs=specs,
        out_specs=[vmem] * len(outs),
        scratch_shapes=list(scratch),
        compiler_params=pltpu.CompilerParams(vmem_limit_bytes=vmem_mib * 2 ** 20),
    )


def solution(mesh):
    nx, ny = mesh.shape["gx"], mesh.shape["gy"]

    def pairs(count, parity):
        return [(i, (i + 1) % count if i % 2 == parity else (i - 1) % count) for i in range(count)]

    def body(fields, solid_mask):
        parity = jnp.stack([lax.axis_index("gx") % 2, lax.axis_index("gy") % 2]).astype(jnp.int32)
        ymsg = (NF, 2, NX, NY)
        parts = [(-(count * MSG) // 8 * -8, NY) for count in (FIRST, NZ - FIRST)]
        q, m = fields, solid_mask.astype(F32)
        yb, ya, xa, xb, xb2 = call(pack_kernel, [ymsg, ymsg, (NZ * MSG, NY)] + parts, inputs=2)(parity, q, m)
        yb = lax.ppermute(yb, "gy", pairs(ny, 1))
        ya = lax.ppermute(ya, "gy", pairs(ny, 0))
        xb = lax.ppermute(xb, "gx", pairs(nx, 1))
        xb2 = lax.ppermute(xb2, "gx", pairs(nx, 1))
        xa = lax.ppermute(xa, "gx", pairs(nx, 0))
        t, ts, ca, cb = call(strip_kernel, [(NF, 4, NX, NY), (4, NX, NY), (4 * MSG, NY), (4 * MSG, NY)],
                             inputs=2)(parity, yb, ya)
        w = y_weights()
        w = call(fetch_kernel, [jax.ShapeDtypeStruct(a.shape, a.dtype) for a in w],
                 [pltpu.SemaphoreType.DMA((2,))], hbm=3)(parity, *w, cb)
        cb = lax.ppermute(cb, "gx", pairs(nx, 1))
        ca = lax.ppermute(ca, "gx", pairs(nx, 0))
        wide = (NF, NZ, ROWS, NY)
        narrow = (NF, 8, ROWS, NY)
        scratch = [wide] * 3 + [(NZ, ROWS, NY)] + [narrow] * 3 + [(4, ROWS, NY)]
        scratch += [(NF, NZ, 48, 2 * NY), (NF, 4, 48, 2 * NY)]
        scratch = [pltpu.VMEM(s, F32) for s in scratch]
        parts = []
        for _, tiles, _ in EARLY.values():
            parts += [(NF, NZ, 8 * tiles, NY), (NF, 4, 8 * tiles, NY)]
        early = call(early_kernel, parts, scratch, inputs=6, vmem_mib=32)(parity, q, m, t, ts, *w)
        out, = call(main_kernel, [(NF, NZ, NX, NY)], scratch, inputs=11 + len(parts), vmem_mib=32)(
            parity, q, m, xa, xb, xb2, t, ts, ca, cb, *w, *early)
        return out

    return jax.shard_map(
        body,
        mesh=mesh,
        in_specs=(P(None, None, "gx", "gy"), P(None, "gx", "gy")),
        out_specs=P(None, None, "gx", "gy"),
        check_vma=False,
    )
```
